768 devices in a mesh: edata: 4 (over x), expert: 16 (over y, core), tensor: 12 (over z).
Axes of the slice: x: 4, y: 8, z: 12, core: 2. Of those that a mesh axis runs over, the one named last changes fastest.
Arguments:
- grad_out: bfloat16 [2048, 4096], P(('edata', 'expert')), may hold values from -6 to 6
- gates: bfloat16 [2048, 8], P(('edata', 'expert')), may hold values from 0.019897461 to 0.5
- expert_ids: int32 [2048, 8], P(('edata', 'expert')), may hold values from 0 to 31, all different within a row; in each aligned block of 32 rows (0 to 31, 32 to 63, ...) at most 12 rows name the same one
- hidden: bfloat16 [4, 16, 32, 12, 1536], P('edata', None, 'expert', None, 'tensor'), may hold values from -0.19921875 to 0.19921875
- down_weight: bfloat16 [32, 1536, 4096], P('expert', 'tensor'), may hold values from -0.15625 to 0.15625
- moment_one: bfloat16 [4096, 32, 1536], P('edata', 'expert', 'tensor'), may hold values from -0.119628906 to 0.119628906
- moment_two: float32 [4096, 32, 1536], P('edata', 'expert', 'tensor'), may hold values from 0.0001 to 0.01
Outputs:
- grad_hidden: bfloat16 [4, 16, 32, 12, 1536], P('edata', None, 'expert', None, 'tensor')
- grad_gates: float32 [2048, 8], P(('edata', 'expert'))
- new_weight: bfloat16 [4096, 32, 1536], P('edata', 'expert', 'tensor')
- new_moment_one: bfloat16 [4096, 32, 1536], P('edata', 'expert', 'tensor')
- new_moment_two: float32 [4096, 32, 1536], P('edata', 'expert', 'tensor')
The draws below stay inside these ranges and needn't reach their ends.
Inputs may be any that keep to these rules, and one draw needn't show every extreme that they name: `expert_ids`: each row names 8 different experts. Among the rows of one source block of 32 tokens no expert is named more than 12 times, and in every draw some expert is named exactly 12 times by some block.
All inputs are finite; a program needn't handle non-finite values.
Results may differ from the reference program's by a relative error of at most 0.012.
Values may be sent and summed in bfloat16 or wider, within the bound.
No kernel may reach another device: no remote copies, remote signals or barrier semaphores. Data moves between devices by JAX's collectives and lax.ppermute only.
A program may use at most 128 MiB of HBM per device.

```python
import math
import jax
import jax.numpy as jnp
import numpy as np
from jax import lax

D = 4096
FF = 1536
K = 8
TOK_DEV = 32
EXPERTS = 32
CAP_E = 12
TOKENS = 2048
N_EDATA = 4
N_EXPERT = 16


def block_scale(key, extent, pieces, smallest, high):
    def one(dim, blocks):
        steps = jax.random.uniform(jax.random.fold_in(jax.random.fold_in(key, 6), dim), (blocks,), jnp.float32, smallest / len(pieces), high / len(pieces))
        return jnp.repeat(jnp.exp(steps), extent[dim] // blocks).reshape((-1,) + (1,) * (len(extent) - dim - 1))

    gain = one(*pieces[0])
    for cut in pieces[1:]:
        gain = gain * one(*cut)
    return gain


def deal_out(own_key, own, number, rows, number_of, top, bound, slope):
    sequence = jax.random.permutation(own_key, number_of)
    packed, usual = shares(number_of, rows * top, bound, slope, True), shares(number_of, rows * top, bound, slope, False)
    places = jnp.arange(number_of)

    def named(sizes, rotation):
        used = int((sizes > 0).sum())
        fixed = max(1, used // 4)
        shifted = fixed + (places - fixed + rotation * (used - fixed)) % max(1, number_of - fixed)
        return jnp.zeros((number_of,), jnp.int32).at[sequence[jnp.where(places < fixed, places, shifted)]].set(jnp.asarray(sizes, jnp.int32))

    sizes = jnp.where(number % 4 == 0, named(packed, number // 4), named(usual, number - number // 4 - 1))
    mixed = jax.random.permutation(jax.random.fold_in(own, 3), number_of)
    source_of, sink = mixed[0:number_of // 2 * 2:2], mixed[1:number_of // 2 * 2:2]
    margin = jnp.minimum(sizes[source_of] - 1, bound - sizes[sink]) // 2
    margin = jnp.where((source_of == sequence[0]) | (sink == sequence[0]) | (sizes[sink] == 0), 0, jnp.maximum(margin, 0))
    shifted = jax.random.randint(jax.random.fold_in(own, 4), (number_of // 2,), 0, 1 << 20) % (margin + 1)
    sizes = sizes.at[source_of].add(-shifted).at[sink].add(shifted)
    items = jnp.searchsorted(jnp.cumsum(sizes), jnp.arange(rows * top), side="right").astype(jnp.int32)
    table = items.reshape(top, rows).T
    table = table[jax.random.permutation(jax.random.fold_in(own, 1), rows)]
    rotation = jax.random.randint(jax.random.fold_in(own, 2), (rows, 1), 0, top)
    return jnp.take_along_axis(table, (jnp.arange(top)[None, :] + rotation) % top, axis=1)


def shares(number_of, total, most, slope, full):
    weights = [(1 << 20) // math.isqrt(grade ** slope) + 1 for grade in range(1, number_of + 1)]
    largest = most if full else min(most, max(-(-total // number_of), total * weights[0] // sum(weights)))
    least = 1 if total - largest >= number_of - 1 else 0
    counts, spare = [largest] + [least] * (number_of - 1), total - largest - least * (number_of - 1)
    while spare > 0:
        free = [i for i in range(1, number_of) if counts[i] < largest] or [i for i in range(1, number_of) if counts[i] < most]
        mass, remaining = sum([weights[i] for i in free]), spare
        for i in free:
            addition = min(most - counts[i], max(1, remaining * weights[i] // mass), spare)
            counts[i] = counts[i] + addition
            spare = spare - addition
    return np.array(counts)


def scatter_about(key, dims, width, reach, cuts=(), kind=jnp.bfloat16):
    entries = jax.random.normal(key, dims, jnp.float32) * width
    if len(cuts) > 0:
        entries = block_scale(key, dims, cuts, -0.22, 0.18) * entries
    return jnp.clip(entries, min=-reach, max=reach).astype(kind)


def setup_inputs(seed: int = 0) -> dict:
    seeds = jax.random.split(jax.random.key(seed), 8)
    grad_out = scatter_about(seeds[0], (TOKENS, D), 1.0, 6.0, ((0, 64),))
    gates = jnp.clip(jnp.exp(math.log(0.5) - 3.224016 * jax.random.uniform(seeds[1], (TOKENS, K), jnp.float32) ** block_scale(seeds[1], (TOKENS, K), ((0, 64),), -0.2, 0.2)), 0.019897461, 0.5).astype(jnp.bfloat16)
    expert_ids_keys = jax.random.split(jax.random.fold_in(seeds[2], 1), TOKENS // TOK_DEV)
    expert_ids_turns = jax.random.permutation(jax.random.fold_in(seeds[2], 3), TOKENS // TOK_DEV)
    expert_ids = jax.vmap(lambda own, number: deal_out(jax.random.fold_in(seeds[2], 2), own, number, TOK_DEV, EXPERTS, K, CAP_E, 2))(expert_ids_keys, expert_ids_turns).reshape((TOKENS, K))
    hidden = scatter_about(seeds[3], (N_EDATA, N_EXPERT, EXPERTS, CAP_E, FF), 0.03, 0.19921875, ((0, 4), (2, 16), (4, 12)))
    down_weight = scatter_about(seeds[4], (EXPERTS, FF, D), FF ** -0.5, 0.15625, ((0, 16), (1, 12)))
    moment_one = scatter_about(seeds[5], (D, EXPERTS, FF), 0.02, 0.119628906, ((0, 4), (1, 16), (2, 12)))
    moment_two = jnp.clip(jnp.exp(math.log(0.01) - 4.6051702 * jax.random.uniform(seeds[6], (D, EXPERTS, FF), jnp.float32) ** block_scale(seeds[6], (D, EXPERTS, FF), ((0, 4), (1, 16), (2, 12)), -0.2, 0.2)), 0.0001, 0.01)
    return dict(grad_out=grad_out, gates=gates, expert_ids=expert_ids, hidden=hidden, down_weight=down_weight, moment_one=moment_one, moment_two=moment_two)


beta_one = 0.9
beta_two = 0.999
adam_eps = 1e-08
learn_rate = 0.01
corr_two = 0.6323045752

def route_slots(expert_ids, experts, capacity):
    flat_ids = expert_ids.reshape(-1).astype(jnp.int32)
    onehot = (flat_ids[:, None] == jnp.arange(experts, dtype=jnp.int32)[None, :]).astype(jnp.int32)
    before = lax.optimization_barrier(jnp.sum((jnp.cumsum(onehot, axis=0) - onehot) * onehot, axis=1))
    slot_index = flat_ids * capacity + before
    return slot_index[None, :] == jnp.arange(experts * capacity, dtype=jnp.int32)[:, None]

def reference(grad_out, gates, expert_ids, hidden, down_weight, moment_one, moment_two):
    sources = N_EDATA * N_EXPERT
    route_ids = expert_ids.reshape(sources, TOK_DEV, K)
    token_grads = grad_out.reshape(sources, TOK_DEV, D)
    token_gates = gates.reshape(sources, TOK_DEV * K)

    def dispatch(inputs):
        ids_here, grads_here, gates_here = inputs
        placed = route_slots(ids_here, EXPERTS, CAP_E)
        per_token = jnp.any(placed.reshape(EXPERTS * CAP_E, TOK_DEV, K), axis=2).astype(jnp.bfloat16)
        slot_rows = jnp.dot(per_token, grads_here, preferred_element_type=jnp.float32).astype(jnp.bfloat16)
        slot_gate = lax.optimization_barrier(jnp.sum(jnp.where(placed, gates_here.astype(jnp.float32)[None, :], jnp.zeros((), jnp.float32)), axis=1))
        return (slot_rows, slot_gate.astype(jnp.bfloat16))
    slot_rows, slot_gate = lax.map(dispatch, (route_ids, token_grads, token_gates))
    slot_rows = jnp.moveaxis(slot_rows.reshape(N_EDATA, N_EXPERT, EXPERTS, CAP_E, D), 2, 0)
    slot_gate = jnp.moveaxis(slot_gate.reshape(N_EDATA, N_EXPERT, EXPERTS, CAP_E), 2, 0)
    saved = jnp.moveaxis(hidden, 2, 0)
    first_in = jnp.moveaxis(moment_one, 1, 0)
    second_in = jnp.moveaxis(moment_two, 1, 0)

    def expert_step(inputs):
        rows_here, gate_here, saved_here, weight_here, first_here, second_here = inputs
        flat_rows = rows_here.reshape(-1, D)
        flat_saved = saved_here.reshape(-1, FF)
        gate_scale = gate_here.reshape(-1, 1).astype(jnp.float32)
        upstream = jnp.dot(flat_rows, weight_here.T, preferred_element_type=jnp.float32)
        grad_hidden = (gate_scale * upstream).astype(jnp.bfloat16)
        slot_grad = lax.optimization_barrier(jnp.sum(flat_saved.astype(jnp.float32) * upstream, axis=1))
        weighted = (gate_scale * flat_rows.astype(jnp.float32)).astype(jnp.bfloat16)
        per_replica = jnp.einsum('ird,irf->idf', weighted.reshape(N_EDATA, -1, D).astype(jnp.float32), flat_saved.reshape(N_EDATA, -1, FF).astype(jnp.float32))
        rounded = lax.optimization_barrier(per_replica.astype(jnp.bfloat16))
        grad = lax.optimization_barrier(jnp.sum(rounded.astype(jnp.float32), axis=0))
        moment_new = beta_one * first_here.astype(jnp.float32) + (1.0 - beta_one) * grad
        second_new = beta_two * second_here + (1.0 - beta_two) * grad * grad
        update = moment_new / (jnp.sqrt(second_new / corr_two) + adam_eps)
        weight_new = (weight_here.T.astype(jnp.float32) - learn_rate * update).astype(jnp.bfloat16)
        return (grad_hidden.reshape(saved_here.shape), slot_grad.reshape(gate_here.shape), weight_new, moment_new.astype(jnp.bfloat16), second_new)
    grad_hidden, slot_grad, weight_new, first_new, second_new = lax.map(expert_step, (slot_rows, slot_gate, saved, down_weight, first_in, second_in))
    grad_hidden = jnp.moveaxis(grad_hidden, 0, 2)
    slot_grad = jnp.moveaxis(slot_grad, 0, 2).reshape(sources, EXPERTS * CAP_E)

    def gather_back(inputs):
        ids_here, grads_here = inputs
        placed = route_slots(ids_here, EXPERTS, CAP_E)
        return lax.optimization_barrier(jnp.sum(jnp.where(placed, grads_here[:, None], jnp.zeros((), jnp.float32)), axis=0))
    grad_gates = lax.map(gather_back, (route_ids, slot_grad)).reshape(TOKENS, K)
    return (grad_hidden, grad_gates, jnp.moveaxis(weight_new, 0, 1), jnp.moveaxis(first_new, 0, 1), jnp.moveaxis(second_new, 0, 1))
```

```python
import functools

import jax
import jax.numpy as jnp
from jax import lax
from jax.experimental import pallas as pl
from jax.experimental.pallas import tpu as pltpu
from jax.sharding import Mesh, PartitionSpec as P

beta_one = 0.9
beta_two = 0.999
adam_eps = 1e-08
learn_rate = 0.01
corr_two = 0.6323045752

F32 = jnp.float32
BF16 = jnp.bfloat16
LANES = 128
PARAMS = pltpu.CompilerParams(vmem_limit_bytes=40 * 1024 * 1024)


def dot(a, b, over, precision=None):
    return lax.dot_general(
        a, b, (((over[0],), (over[1],)), ((), ())), precision=precision, preferred_element_type=F32
    )


def expert_base():
    return ((lax.axis_index("ey") * 2 + lax.axis_index("core")) * 2).astype(F32)


def routed(meta, base, tokens, rows):
    count = meta.shape[0]
    meta = meta.astype(F32)
    ids, gates = meta[:, :8], meta[:, 8:16]
    hits = [ids == base + e for e in range(2)]
    named = [jnp.sum(jnp.where(h, 1.0, 0.0), axis=1, keepdims=True) for h in hits]
    gate = [jnp.sum(jnp.where(h, gates, 0.0), axis=1, keepdims=True) for h in hits]
    lane = lax.broadcasted_iota(jnp.int32, (count, LANES), 1)
    marks = jnp.where(lane == 0, named[0], jnp.where(lane == 1, named[1], 0.0)).astype(BF16)
    row_i = lax.broadcasted_iota(jnp.int32, (count, count), 0)
    col_i = lax.broadcasted_iota(jnp.int32, (count, count), 1)
    earlier = ((row_i // tokens == col_i // tokens) & (col_i < row_i)).astype(F32).astype(BF16)
    rank = dot(earlier, marks, (1, 0))
    block = (lax.broadcasted_iota(jnp.int32, (count, 1), 0) // tokens).astype(F32)
    slot_rows = (count // tokens) * rows
    slot_lane = lax.broadcasted_iota(jnp.int32, (count, slot_rows), 1).astype(F32)
    keys = [
        jnp.where(named[e] > 0.5, block * rows + 2.0 * rank[:, e : e + 1] + e, -1.0)
        for e in range(2)
    ]
    onehot = ((slot_lane == keys[0]) | (slot_lane == keys[1])).astype(F32).astype(BF16)
    return onehot, gate


def by_expert(hid):
    odd = lax.broadcasted_iota(jnp.int32, hid.shape, 0) % 2
    hid = hid.astype(F32)
    return jnp.concatenate(
        [jnp.where(odd == 0, hid, 0.0), jnp.where(odd == 1, hid, 0.0)], axis=1
    ).astype(BF16)


def gate_lanes(gate):
    return jnp.concatenate([jnp.broadcast_to(g, (g.shape[0], LANES)) for g in gate], axis=1)


def own_kernel(tokens, rows, width, part, mine, theirs, weight, hid, grad_hidden, gate_part, grad):
    core = lax.axis_index("core")
    base = expert_base()
    column = pl.multiple_of(lax.axis_index("edata") * part, LANES)
    total = None
    gates_out = None
    count = mine.shape[0]
    slots = count // tokens * rows
    for rel, ref in enumerate((mine, theirs)):
        side = core if rel == 0 else 1 - core
        onehot, gate = routed(ref[:, width : width + LANES], base, tokens, rows)
        saved = dot(onehot, by_expert(hid[rel * slots : (rel + 1) * slots, :]), (1, 0))
        up = dot(ref[:, :width], weight[...], (1, 1))
        scale = gate_lanes(gate)
        picked = dot(onehot, (scale * up).astype(BF16), (0, 0))
        even = lax.broadcasted_iota(jnp.int32, (slots, LANES), 0) % 2 == 0
        picked = jnp.where(even, picked[:, :LANES], picked[:, LANES:]).astype(BF16)
        for block in range(count // tokens):
            grad_hidden[block, side] = picked[block * rows : (block + 1) * rows]
        prod = saved * up
        column_e = [
            jnp.sum(prod[:, e * LANES : (e + 1) * LANES], axis=1, keepdims=True) for e in range(2)
        ]
        lane = lax.broadcasted_iota(jnp.int32, (count, LANES), 1)
        tok = lax.broadcasted_iota(jnp.int32, (count, LANES), 0) % tokens
        spread = jnp.zeros((count, LANES), F32)
        for e in range(2):
            spread = jnp.where(lane == (side * 2 + e) * tokens + tok, column_e[e], spread)
        block_of = lax.broadcasted_iota(jnp.int32, (count // tokens, count), 1) // tokens
        block_row = lax.broadcasted_iota(jnp.int32, (count // tokens, count), 0)
        pick = (block_of == block_row).astype(F32)
        piece = dot(pick, spread, (1, 0), lax.Precision.HIGHEST)
        gates_out = piece if gates_out is None else gates_out + piece
        scaled = (scale * saved).astype(BF16)
        term = dot(ref[:, pl.ds(column, part)], scaled, (0, 0))
        total = term if total is None else total + term
    gate_part[...] = gates_out
    grad[...] = total


def adam_kernel(
    tokens, rows, part, mine, theirs, grad, hid, weight, one, two,
    new_weight, new_one, new_two, grad_rows, weight_rows,
):
    base = expert_base()
    total = grad[...]
    blocks = mine.shape[0]
    others = mine.shape[1] // tokens
    slots = blocks * rows
    for rel, ref in enumerate((mine, theirs)):
        for other in range(others):
            at = pl.ds(other * tokens, tokens)
            meta = ref[:, at, part : part + LANES].reshape(blocks * tokens, LANES)
            onehot, gate = routed(meta, base, tokens, rows)
            saved = dot(
                onehot, by_expert(hid[other, rel * slots : (rel + 1) * slots, :]), (1, 0)
            )
            scaled = (gate_lanes(gate) * saved).astype(BF16)
            toks = ref[:, at, :part].reshape(blocks * tokens, part)
            total = total + dot(toks, scaled, (0, 0))
    column = pl.multiple_of(lax.axis_index("edata") * part, LANES)
    for e in range(2):
        grad_rows[pl.ds(e, part, 2), :] = total[:, e * LANES : (e + 1) * LANES]
        piece = weight[e * LANES : (e + 1) * LANES, pl.ds(column, part)].astype(F32)
        weight_rows[pl.ds(e, part, 2), :] = piece.T
    g = grad_rows[...]
    first = beta_one * one[...].astype(F32) + (1.0 - beta_one) * g
    second = beta_two * two[...] + (1.0 - beta_two) * g * g
    update = first / (jnp.sqrt(second / corr_two) + adam_eps)
    new_weight[...] = (weight_rows[...] - learn_rate * update).astype(BF16)
    new_one[...] = first.astype(BF16)
    new_two[...] = second


def cost(tokens, terms, moved):
    return pl.CostEstimate(flops=2 * tokens * terms, bytes_accessed=moved, transcendentals=0)


def shards(grad_out, gates, expert_ids, hidden, down_weight, moment_one, moment_two):
    tokens, width = grad_out.shape
    choices = gates.shape[1]
    blocks, replicas = lax.axis_size("ey"), lax.axis_size("edata")
    held, capacity = hidden.shape[2], hidden.shape[3]
    rows = held * capacity
    part = width // replicas
    index, core = lax.axis_index("edata"), lax.axis_index("core")
    swap = [(0, 1), (1, 0)]

    meta = jnp.concatenate(
        [expert_ids.astype(BF16), gates, jnp.zeros((tokens, LANES - 2 * choices), BF16)], axis=1
    )
    own = lax.all_gather(jnp.concatenate([grad_out, meta], axis=1), "ey", axis=0, tiled=True)
    own_other = lax.ppermute(own, "core", swap)

    to_replicas = jnp.stack(
        [
            jnp.concatenate([grad_out[:, j * part : (j + 1) * part], meta], axis=1)
            for j in range(replicas)
        ]
    )
    from_replicas = lax.all_to_all(to_replicas, "edata", 0, 0, tiled=True)
    rest = lax.dynamic_slice_in_dim(
        jnp.concatenate([from_replicas, from_replicas[:-1]], axis=0), index + 1, replicas - 1, 0
    ).reshape((replicas - 1) * tokens, part + LANES)
    saved = jnp.transpose(hidden[0], (0, 2, 1, 3)).reshape(blocks, 2, rows, LANES)
    saved = jnp.where(core == 0, saved, saved[:, ::-1])
    saved = jnp.transpose(saved, (1, 0, 2, 3)).reshape(2 * blocks * rows, LANES)
    saved_all = lax.all_to_all(
        jnp.broadcast_to(saved[None], (replicas,) + saved.shape), "edata", 0, 0, tiled=True
    )
    saved_rest = lax.dynamic_slice_in_dim(
        jnp.concatenate([saved_all, saved_all[:-1]], axis=0), index + 1, replicas - 1, 0
    )

    rest, saved_rest = lax.optimization_barrier((rest, saved_rest))
    rest = lax.all_gather(rest, "ey", axis=0)

    weight = down_weight.reshape(held * LANES, width)
    grad_hidden, gate_part, grad = pl.pallas_call(
        functools.partial(own_kernel, tokens, rows, width, part),
        out_shape=(
            jax.ShapeDtypeStruct((blocks, 2, rows, LANES), BF16),
            jax.ShapeDtypeStruct((blocks, LANES), F32),
            jax.ShapeDtypeStruct((part, held * LANES), F32),
        ),
        compiler_params=PARAMS,
        cost_estimate=cost(2 * blocks * tokens, (width + part) * held * LANES, 8 << 20),
        name="own_tokens",
    )(own, own_other, weight, saved)

    planes = lax.axis_size("tensor")
    gate_all = lax.all_to_all(
        jnp.broadcast_to(gate_part[None], (planes,) + gate_part.shape), "tensor", 0, 0, tiled=True
    )
    gate_sum = jnp.sum(gate_all, axis=0)
    rest, grad, gate_sum = lax.optimization_barrier((rest, grad, gate_sum))
    rest_other = lax.ppermute(rest, "core", swap)
    gate_sum = gate_sum.reshape(2 * blocks, 1, held * tokens)
    gate_home = lax.all_to_all(gate_sum, ("ey", "core"), 0, 0, tiled=True)
    by_token = gate_home.reshape(2 * blocks * held, tokens)
    experts = lax.broadcasted_iota(jnp.int32, (2 * blocks * held, tokens, choices), 0)
    grad_gates = jnp.sum(
        jnp.where(experts == expert_ids[None], by_token[:, :, None], 0.0), axis=0
    )

    flat = (part * held, LANES)
    new_weight, new_one, new_two = pl.pallas_call(
        functools.partial(adam_kernel, tokens, rows, part),
        out_shape=(
            jax.ShapeDtypeStruct(flat, BF16),
            jax.ShapeDtypeStruct(flat, BF16),
            jax.ShapeDtypeStruct(flat, F32),
        ),
        scratch_shapes=[pltpu.VMEM(flat, F32), pltpu.VMEM(flat, F32)],
        compiler_params=PARAMS,
        cost_estimate=cost(
            2 * blocks * tokens * (replicas - 1), part * held * LANES, 12 << 20
        ),
        name="adam",
    )(
        rest, rest_other, grad, saved_rest, weight,
        moment_one.reshape(flat), moment_two.reshape(flat),
    )
    grad_hidden = jnp.transpose(
        grad_hidden.reshape(1, 2 * blocks, capacity, held, LANES), (0, 1, 3, 2, 4)
    )
    shape = moment_one.shape
    return (
        grad_hidden, grad_gates, new_weight.reshape(shape), new_one.reshape(shape),
        new_two.reshape(shape),
    )


def solution(mesh):
    replicas, groups, planes = mesh.devices.shape
    fine = Mesh(
        mesh.devices.reshape(replicas, groups // 2, 2, planes), ("edata", "ey", "core", "tensor")
    )
    expert = ("ey", "core")
    block = P(("edata", "ey", "core"), None)
    state = P("edata", expert, "tensor")
    saved = P("edata", None, expert, None, "tensor")
    return jax.shard_map(
        shards,
        mesh=fine,
        in_specs=(block, block, block, saved, P(expert, "tensor", None), state, state),
        out_specs=(saved, block, state, state, state),
        check_vma=False,
    )
```

```python
import functools

import jax
import jax.numpy as jnp
from jax import lax
from jax.experimental import pallas as pl
from jax.experimental.pallas import tpu as pltpu
from jax.sharding import Mesh, PartitionSpec as P

beta_one = 0.9
beta_two = 0.999
adam_eps = 1e-08
learn_rate = 0.01
corr_two = 0.6323045752

F32 = jnp.float32
BF16 = jnp.bfloat16
LANES = 128
PARAMS = pltpu.CompilerParams(vmem_limit_bytes=40 * 1024 * 1024)


def dot(a, b, over, precision=None):
    return lax.dot_general(
        a, b, (((over[0],), (over[1],)), ((), ())), precision=precision, preferred_element_type=F32
    )


def expert_base():
    return ((lax.axis_index("ey") * 2 + lax.axis_index("core")) * 2).astype(F32)


def routed(meta, base, tokens, rows):
    count = meta.shape[0]
    meta = meta.astype(F32)
    ids, gates = meta[:, :8], meta[:, 8:16]
    hits = [ids == base + e for e in range(2)]
    named = [jnp.sum(jnp.where(h, 1.0, 0.0), axis=1, keepdims=True) for h in hits]
    gate = [jnp.sum(jnp.where(h, gates, 0.0), axis=1, keepdims=True) for h in hits]
    lane = lax.broadcasted_iota(jnp.int32, (count, LANES), 1)
    marks = jnp.where(lane == 0, named[0], jnp.where(lane == 1, named[1], 0.0)).astype(BF16)
    row_i = lax.broadcasted_iota(jnp.int32, (count, count), 0)
    col_i = lax.broadcasted_iota(jnp.int32, (count, count), 1)
    earlier = ((row_i // tokens == col_i // tokens) & (col_i < row_i)).astype(F32).astype(BF16)
    rank = dot(earlier, marks, (1, 0))
    block = (lax.broadcasted_iota(jnp.int32, (count, 1), 0) // tokens).astype(F32)
    slot_rows = (count // tokens) * rows
    slot_lane = lax.broadcasted_iota(jnp.int32, (count, slot_rows), 1).astype(F32)
    keys = [
        jnp.where(named[e] > 0.5, block * rows + 2.0 * rank[:, e : e + 1] + e, -1.0)
        for e in range(2)
    ]
    onehot = ((slot_lane == keys[0]) | (slot_lane == keys[1])).astype(F32).astype(BF16)
    return onehot, gate


def by_expert(hid):
    odd = lax.broadcasted_iota(jnp.int32, hid.shape, 0) % 2
    hid = hid.astype(F32)
    return jnp.concatenate(
        [jnp.where(odd == 0, hid, 0.0), jnp.where(odd == 1, hid, 0.0)], axis=1
    ).astype(BF16)


def gate_lanes(gate):
    return jnp.concatenate([jnp.broadcast_to(g, (g.shape[0], LANES)) for g in gate], axis=1)


def own_kernel(tokens, rows, width, *refs):
    mine, theirs = refs[:9], refs[9:14]
    weight, hid, grad_hidden, gate_part, grad, toks = refs[14:]
    core, line = lax.axis_index("core"), lax.axis_index("ey")
    base = expert_base()
    blocks = grad_hidden.shape[0]
    count = blocks * tokens
    at = 0
    for ref in mine + theirs:
        toks[at : at + ref.shape[0], :] = ref[...]
        at += ref.shape[0]
    where = [(line + step) % blocks for step in arrival(blocks)]
    gates_out = None
    scaled = []
    for rel in range(2):
        side = core if rel == 0 else 1 - core
        here = slice(rel * count, (rel + 1) * count)
        onehot, gate = routed(toks[here, width : width + LANES], base, tokens, rows)
        slots = jnp.concatenate([hid[block, side].astype(F32) for block in where], axis=0)
        saved = dot(onehot, by_expert(slots), (1, 0))
        up = dot(toks[here, :width], weight[...], (1, 1))
        scale = gate_lanes(gate)
        scaled.append((scale * saved).astype(BF16))
        picked = dot(onehot, (scale * up).astype(BF16), (0, 0))
        even = lax.broadcasted_iota(jnp.int32, (blocks * rows, LANES), 0) % 2 == 0
        picked = jnp.where(even, picked[:, :LANES], picked[:, LANES:])
        for order, block in enumerate(where):
            grad_hidden[block, side] = picked[order * rows : (order + 1) * rows].astype(BF16)
        prod = saved * up
        lane = lax.broadcasted_iota(jnp.int32, (count, LANES), 1)
        tok = lax.broadcasted_iota(jnp.int32, (count, LANES), 0) % tokens
        spread = jnp.zeros((count, LANES), F32)
        for e in range(2):
            total = jnp.sum(prod[:, e * LANES : (e + 1) * LANES], axis=1, keepdims=True)
            spread = jnp.where(lane == (side * 2 + e) * tokens + tok, total, spread)
        order = lax.broadcasted_iota(jnp.int32, (blocks, count), 1) // tokens
        away = jnp.where(order % 2 == 1, -((order + 1) // 2), order // 2)
        row = lax.broadcasted_iota(jnp.int32, (blocks, count), 0)
        pick = ((line + away + blocks) % blocks == row).astype(F32)
        piece = dot(pick, spread, (1, 0), lax.Precision.HIGHEST)
        gates_out = piece if gates_out is None else gates_out + piece
    gate_part[...] = gates_out
    scaled = jnp.concatenate(scaled, axis=0)
    part = grad.shape[0]
    column = pl.multiple_of(lax.axis_index("edata") * part, LANES)
    grad[...] = dot(toks[:, pl.ds(column, part)], scaled, (0, 0))


def arrival(blocks):
    steps = [0]
    for away in range(1, blocks // 2):
        steps += [blocks - away, away]
    return steps + [blocks // 2]


def adam_kernel(
    tokens, rows, part, mine, theirs, grad, hid, weight, one, two,
    new_weight, new_one, new_two, grad_rows, weight_rows,
):
    base = expert_base()
    total = grad[...]
    blocks = mine.shape[0]
    others = mine.shape[1] // tokens
    slots = blocks * rows
    for rel, ref in enumerate((mine, theirs)):
        for other in range(others):
            at = pl.ds(other * tokens, tokens)
            meta = ref[:, at, part : part + LANES].reshape(blocks * tokens, LANES)
            onehot, gate = routed(meta, base, tokens, rows)
            saved = dot(
                onehot, by_expert(hid[other, rel * slots : (rel + 1) * slots, :]), (1, 0)
            )
            scaled = (gate_lanes(gate) * saved).astype(BF16)
            toks = ref[:, at, :part].reshape(blocks * tokens, part)
            total = total + dot(toks, scaled, (0, 0))
    column = pl.multiple_of(lax.axis_index("edata") * part, LANES)
    for e in range(2):
        grad_rows[pl.ds(e, part, 2), :] = total[:, e * LANES : (e + 1) * LANES]
        piece = weight[e * LANES : (e + 1) * LANES, pl.ds(column, part)].astype(F32)
        weight_rows[pl.ds(e, part, 2), :] = piece.T
    g = grad_rows[...]
    first = beta_one * one[...].astype(F32) + (1.0 - beta_one) * g
    second = beta_two * two[...] + (1.0 - beta_two) * g * g
    update = first / (jnp.sqrt(second / corr_two) + adam_eps)
    new_weight[...] = (weight_rows[...] - learn_rate * update).astype(BF16)
    new_one[...] = first.astype(BF16)
    new_two[...] = second


def cost(tokens, terms, moved):
    return pl.CostEstimate(flops=2 * tokens * terms, bytes_accessed=moved, transcendentals=0)


def gathered(own, between):
    size, half = lax.axis_size("ey"), own.shape[0] // 2
    ahead = [(i, (i + 1) % size) for i in range(size)]
    back = [(i, (i - 1) % size) for i in range(size)]
    swap = [(0, 1), (1, 0)]
    mine, theirs = [own], [lax.ppermute(own, "core", swap)]
    up = down = own
    for step in range(1, size // 2):
        up, down = lax.ppermute(up, "ey", ahead), lax.ppermute(down, "ey", back)
        up, down = between(step, up, down)
        mine += [up, down]
        theirs.append(lax.ppermute(jnp.concatenate([up, down], axis=0), "core", swap))
    up, down = lax.ppermute(up[:half], "ey", ahead), lax.ppermute(down[half:], "ey", back)
    mine += [up, down]
    theirs.append(lax.ppermute(jnp.concatenate([up, down], axis=0), "core", swap))
    return mine, theirs


def shards(grad_out, gates, expert_ids, hidden, down_weight, moment_one, moment_two):
    tokens, width = grad_out.shape
    choices = gates.shape[1]
    blocks, replicas, planes = (lax.axis_size(n) for n in ("ey", "edata", "tensor"))
    held, capacity = hidden.shape[2], hidden.shape[3]
    rows = held * capacity
    part = width // replicas
    index, core = lax.axis_index("edata"), lax.axis_index("core")

    meta = jnp.concatenate(
        [expert_ids.astype(BF16), gates, jnp.zeros((tokens, LANES - 2 * choices), BF16)], axis=1
    )
    to_replicas = jnp.stack(
        [
            jnp.concatenate([grad_out[:, j * part : (j + 1) * part], meta], axis=1)
            for j in range(replicas)
        ]
    )
    from_replicas = lax.all_to_all(to_replicas, "edata", 0, 0, tiled=True)
    saved = jnp.transpose(hidden[0], (0, 2, 1, 3)).reshape(blocks, 2, rows, LANES)
    by_side = jnp.where(core == 0, saved, saved[:, ::-1])
    by_side = jnp.transpose(by_side, (1, 0, 2, 3)).reshape(2 * blocks * rows, LANES)
    by_side = jnp.broadcast_to(by_side[None], (replicas,) + by_side.shape)

    def not_own(block):
        twice = jnp.concatenate([block, block[:-1]], axis=0)
        return lax.dynamic_slice_in_dim(twice, index + 1, replicas - 1, 0)

    held_back = {}

    def between(step, up, down):
        if step == 1:
            side, tokens_in, up, down = lax.optimization_barrier((by_side, from_replicas, up, down))
            rest = not_own(tokens_in).reshape((replicas - 1) * tokens, part + LANES)
            held_back["rest"] = lax.all_gather(rest, "ey", axis=0)
            held_back["saved"] = lax.all_to_all(side, "edata", 0, 0, tiled=True)
        if step == 3:
            held_back["saved"], up, down = lax.optimization_barrier((held_back["saved"], up, down))
        return up, down

    mine, theirs = gathered(jnp.concatenate([grad_out, meta], axis=1), between)
    rest, saved_rest = held_back["rest"], not_own(held_back["saved"])
    weight = down_weight.reshape(held * LANES, width)
    every = 2 * blocks * tokens
    grad_hidden, gate_part, grad = pl.pallas_call(
        functools.partial(own_kernel, tokens, rows, width),
        out_shape=(
            jax.ShapeDtypeStruct((blocks, 2, rows, LANES), BF16),
            jax.ShapeDtypeStruct((blocks, LANES), F32),
            jax.ShapeDtypeStruct((part, held * LANES), F32),
        ),
        scratch_shapes=[pltpu.VMEM((every, width + LANES), BF16)],
        compiler_params=PARAMS,
        cost_estimate=cost(every, (width + part) * held * LANES, 8 << 20),
        name="own_tokens",
    )(*mine, *theirs, weight, saved)

    rest, grad, gate_part = lax.optimization_barrier((rest, grad, gate_part))
    rest_other = lax.ppermute(rest, "core", [(0, 1), (1, 0)])
    gate_send = jnp.broadcast_to(
        gate_part.reshape(2 * blocks, 1, held * tokens), (2 * blocks, planes, held * tokens)
    ).reshape(2 * blocks * planes, 1, held * tokens)
    gate_home = lax.all_to_all(gate_send, ("ey", "core", "tensor"), 0, 0, tiled=True)
    flat = (part * held, LANES)
    new_weight, new_one, new_two = pl.pallas_call(
        functools.partial(adam_kernel, tokens, rows, part),
        out_shape=(
            jax.ShapeDtypeStruct(flat, BF16),
            jax.ShapeDtypeStruct(flat, BF16),
            jax.ShapeDtypeStruct(flat, F32),
        ),
        scratch_shapes=[pltpu.VMEM(flat, F32), pltpu.VMEM(flat, F32)],
        compiler_params=PARAMS,
        cost_estimate=cost(every * (replicas - 1), part * held * LANES, 12 << 20),
        name="adam",
    )(
        rest, rest_other, grad, saved_rest, weight,
        moment_one.reshape(flat), moment_two.reshape(flat),
    )
    gate_home, new_one = lax.optimization_barrier((gate_home, new_one))
    by_token = jnp.sum(gate_home.reshape(2 * blocks, planes, held * tokens), axis=1)
    by_token = by_token.reshape(2 * blocks * held, tokens)
    experts = lax.broadcasted_iota(jnp.int32, (2 * blocks * held, tokens, choices), 0)
    grad_gates = jnp.sum(
        jnp.where(experts == expert_ids[None], by_token[:, :, None], 0.0), axis=0
    )
    grad_hidden = jnp.transpose(
        grad_hidden.reshape(1, 2 * blocks, capacity, held, LANES), (0, 1, 3, 2, 4)
    )
    shape = moment_one.shape
    return (
        grad_hidden, grad_gates, new_weight.reshape(shape), new_one.reshape(shape),
        new_two.reshape(shape),
    )


def solution(mesh):
    replicas, groups, planes = mesh.devices.shape
    fine = Mesh(
        mesh.devices.reshape(replicas, groups // 2, 2, planes), ("edata", "ey", "core", "tensor")
    )
    expert = ("ey", "core")
    block = P(("edata", "ey", "core"), None)
    state = P("edata", expert, "tensor")
    saved = P("edata", None, expert, None, "tensor")
    return jax.shard_map(
        shards,
        mesh=fine,
        in_specs=(block, block, block, saved, P(expert, "tensor", None), state, state),
        out_specs=(saved, block, state, state, state),
        check_vma=False,
    )
```

```python
import functools

import jax
import jax.numpy as jnp
from jax import lax
from jax.experimental import pallas as pl
from jax.experimental.pallas import tpu as pltpu
from jax.sharding import Mesh, PartitionSpec as P

beta_one = 0.9
beta_two = 0.999
adam_eps = 1e-08
learn_rate = 0.01
corr_two = 0.6323045752

F32 = jnp.float32
BF16 = jnp.bfloat16
LANES = 128
PARAMS = pltpu.CompilerParams(vmem_limit_bytes=40 * 1024 * 1024)


def dot(a, b, over, precision=None):
    return lax.dot_general(
        a, b, (((over[0],), (over[1],)), ((), ())), precision=precision, preferred_element_type=F32
    )


def expert_base():
    return ((lax.axis_index("ey") * 2 + lax.axis_index("core")) * 2).astype(F32)


def routed(meta, base, tokens, rows):
    count = meta.shape[0]
    meta = meta.astype(F32)
    ids, gates = meta[:, :8], meta[:, 8:16]
    hits = [ids == base + e for e in range(2)]
    named = [jnp.sum(jnp.where(h, 1.0, 0.0), axis=1, keepdims=True) for h in hits]
    gate = [jnp.sum(jnp.where(h, gates, 0.0), axis=1, keepdims=True) for h in hits]
    lane = lax.broadcasted_iota(jnp.int32, (count, LANES), 1)
    marks = jnp.where(lane == 0, named[0], jnp.where(lane == 1, named[1], 0.0)).astype(BF16)
    row_i = lax.broadcasted_iota(jnp.int32, (count, count), 0)
    col_i = lax.broadcasted_iota(jnp.int32, (count, count), 1)
    earlier = ((row_i // tokens == col_i // tokens) & (col_i < row_i)).astype(F32).astype(BF16)
    rank = dot(earlier, marks, (1, 0))
    block = (lax.broadcasted_iota(jnp.int32, (count, 1), 0) // tokens).astype(F32)
    slot_rows = (count // tokens) * rows
    slot_lane = lax.broadcasted_iota(jnp.int32, (count, slot_rows), 1).astype(F32)
    keys = [
        jnp.where(named[e] > 0.5, block * rows + 2.0 * rank[:, e : e + 1] + e, -1.0)
        for e in range(2)
    ]
    onehot = ((slot_lane == keys[0]) | (slot_lane == keys[1])).astype(F32).astype(BF16)
    return onehot, gate


def by_expert(hid):
    odd = lax.broadcasted_iota(jnp.int32, hid.shape, 0) % 2
    hid = hid.astype(F32)
    return jnp.concatenate(
        [jnp.where(odd == 0, hid, 0.0), jnp.where(odd == 1, hid, 0.0)], axis=1
    ).astype(BF16)


def gate_lanes(gate):
    return jnp.concatenate([jnp.broadcast_to(g, (g.shape[0], LANES)) for g in gate], axis=1)


def own_kernel(
    tokens, rows, planes, toks, meta, weight, hid, grad_hidden, gate_part, grad, up, saved, scaled
):
    step = pl.program_id(0)
    groups = hid.shape[0] // rows
    halves = 2
    count = groups // halves * tokens
    slots = groups // halves * rows
    base = expert_base()

    def matrix(half):
        here = slice(half * count, (half + 1) * count)
        return here, *routed(meta[here, :], base, tokens, rows)

    @pl.when(step == 0)
    def _():
        for half in range(halves):
            here, onehot, gate = matrix(half)
            slot_rows = hid[half * slots : (half + 1) * slots, :]
            mine = dot(onehot, by_expert(slot_rows), (1, 0))
            saved[here, :] = mine
            scaled[here, :] = (gate_lanes(gate) * mine).astype(BF16)
        up[...] = jnp.zeros_like(up)

    up[...] += dot(toks[...], weight[...], (1, 1))
    grad[...] = dot(toks[...], scaled[...], (0, 0)).astype(BF16)

    @pl.when(step == pl.num_programs(0) - 1)
    def _():
        rows_out = None
        for half in range(halves):
            here, onehot, gate = matrix(half)
            upstream = up[here, :]
            picked = dot(onehot, (gate_lanes(gate) * upstream).astype(BF16), (0, 0))
            even = lax.broadcasted_iota(jnp.int32, (slots, LANES), 0) % 2 == 0
            picked = jnp.where(even, picked[:, :LANES], picked[:, LANES:])
            grad_hidden[half * slots : (half + 1) * slots, :] = picked.astype(BF16)
            prod = saved[here, :] * upstream
            lane = lax.broadcasted_iota(jnp.int32, (count, LANES), 1)
            tok = lax.broadcasted_iota(jnp.int32, (count, LANES), 0) % tokens
            spread = jnp.zeros((count, LANES), F32)
            for e in range(2):
                total = jnp.sum(prod[:, e * LANES : (e + 1) * LANES], axis=1, keepdims=True)
                spread = jnp.where(lane == e * tokens + tok, total, spread)
            block_of = lax.broadcasted_iota(jnp.int32, (groups, count), 1) // tokens
            row = lax.broadcasted_iota(jnp.int32, (groups, count), 0)
            pick = (block_of + half * (groups // halves) == row).astype(F32)
            piece = dot(pick, spread, (1, 0), lax.Precision.HIGHEST)
            rows_out = piece if rows_out is None else rows_out + piece
        for group in range(groups):
            line = rows_out[group : group + 1, : 2 * tokens]
            for plane in range(planes):
                gate_part[group * planes + plane] = line


def home_kernel(tokens, planes, arrived, ids, out):
    groups = arrived.shape[0] // planes
    total = jnp.zeros(ids.shape, F32)
    named = ids[...]
    for group in range(groups):
        line = arrived[group * planes]
        for plane in range(1, planes):
            line = line + arrived[group * planes + plane]
        for e in range(2):
            value = line[:, e * tokens : (e + 1) * tokens]
            total = jnp.where(named == group * 2 + e, value, total)
    out[...] = total


def adam_kernel(part, grad, weight, one, two, new_weight, new_one, new_two, grad_rows, weight_rows):
    total = grad[...].astype(F32)
    column = pl.multiple_of(lax.axis_index("edata") * part, LANES)
    for e in range(2):
        grad_rows[pl.ds(e, part, 2), :] = total[:, e * LANES : (e + 1) * LANES]
        piece = weight[e * LANES : (e + 1) * LANES, pl.ds(column, part)].astype(F32)
        weight_rows[pl.ds(e, part, 2), :] = piece.T
    g = grad_rows[...]
    first = beta_one * one[...].astype(F32) + (1.0 - beta_one) * g
    second = beta_two * two[...] + (1.0 - beta_two) * g * g
    update = first / (jnp.sqrt(second / corr_two) + adam_eps)
    new_weight[...] = (weight_rows[...] - learn_rate * update).astype(BF16)
    new_one[...] = first.astype(BF16)
    new_two[...] = second


def cost(tokens, terms, moved):
    return pl.CostEstimate(flops=2 * tokens * terms, bytes_accessed=moved, transcendentals=0)


def shards(grad_out, gates, expert_ids, hidden, down_weight, moment_one, moment_two):
    tokens, width = grad_out.shape
    choices = gates.shape[1]
    replicas, planes = lax.axis_size("edata"), lax.axis_size("tensor")
    groups = lax.axis_size("ey") * 2
    held, capacity = hidden.shape[2], hidden.shape[3]
    rows = held * capacity
    part = width // replicas
    every = groups * tokens

    meta = jnp.concatenate(
        [expert_ids.astype(BF16), gates, jnp.zeros((tokens, LANES - 2 * choices), BF16)], axis=1
    )
    toks = lax.all_gather(
        jnp.concatenate([grad_out, meta], axis=1), ("ey", "core"), axis=0, tiled=True
    )
    saved = jnp.transpose(hidden[0], (0, 2, 1, 3)).reshape(groups * rows, LANES)
    weight = down_weight.reshape(held * LANES, width)
    whole = pl.BlockSpec((groups * rows, LANES), lambda d: (0, 0))
    grad_hidden, gate_part, grad = pl.pallas_call(
        functools.partial(own_kernel, tokens, rows, planes),
        grid=(replicas,),
        in_specs=[
            pl.BlockSpec((every, part), lambda d: (0, d)),
            pl.BlockSpec((every, LANES), lambda d: (0, width // LANES)),
            pl.BlockSpec((held * LANES, part), lambda d: (0, d)),
            whole,
        ],
        out_specs=(
            whole,
            pl.BlockSpec((groups * planes, 1, held * tokens), lambda d: (0, 0, 0)),
            pl.BlockSpec((part, held * LANES), lambda d: (d, 0)),
        ),
        out_shape=(
            jax.ShapeDtypeStruct((groups * rows, LANES), BF16),
            jax.ShapeDtypeStruct((groups * planes, 1, held * tokens), F32),
            jax.ShapeDtypeStruct((width, held * LANES), BF16),
        ),
        scratch_shapes=[
            pltpu.VMEM((every, held * LANES), F32),
            pltpu.VMEM((every, held * LANES), F32),
            pltpu.VMEM((every, held * LANES), BF16),
        ],
        compiler_params=PARAMS,
        cost_estimate=cost(every, 2 * width * held * LANES, 8 << 20),
        name="own_tokens",
    )(toks, toks, weight, saved)

    grad = lax.psum_scatter(grad, "edata", scatter_dimension=0, tiled=True)
    gate_home = lax.all_to_all(gate_part, ("ey", "core", "tensor"), 0, 0, tiled=True)
    grad_gates = pl.pallas_call(
        functools.partial(home_kernel, tokens, planes),
        out_shape=jax.ShapeDtypeStruct((choices, tokens), F32),
        compiler_params=PARAMS,
        name="gates_home",
    )(gate_home, expert_ids.T).T

    flat = (part * held, LANES)
    new_weight, new_one, new_two = pl.pallas_call(
        functools.partial(adam_kernel, part),
        out_shape=(
            jax.ShapeDtypeStruct(flat, BF16),
            jax.ShapeDtypeStruct(flat, BF16),
            jax.ShapeDtypeStruct(flat, F32),
        ),
        scratch_shapes=[pltpu.VMEM(flat, F32), pltpu.VMEM(flat, F32)],
        compiler_params=PARAMS,
        cost_estimate=cost(part, held * LANES, 8 << 20),
        name="adam",
    )(grad, weight, moment_one.reshape(flat), moment_two.reshape(flat))
    grad_hidden = jnp.transpose(
        grad_hidden.reshape(1, groups, capacity, held, LANES), (0, 1, 3, 2, 4)
    )
    shape = moment_one.shape
    return (
        grad_hidden, grad_gates, new_weight.reshape(shape), new_one.reshape(shape),
        new_two.reshape(shape),
    )


def solution(mesh):
    replicas, groups, planes = mesh.devices.shape
    fine = Mesh(
        mesh.devices.reshape(replicas, groups // 2, 2, planes), ("edata", "ey", "core", "tensor")
    )
    expert = ("ey", "core")
    block = P(("edata", "ey", "core"), None)
    state = P("edata", expert, "tensor")
    saved = P("edata", None, expert, None, "tensor")
    return jax.shard_map(
        shards,
        mesh=fine,
        in_specs=(block, block, block, saved, P(expert, "tensor", None), state, state),
        out_specs=(saved, block, state, state, state),
        check_vma=False,
    )
```

```python
import functools

import jax
import jax.numpy as jnp
from jax import lax
from jax.experimental import pallas as pl
from jax.experimental.pallas import tpu as pltpu
from jax.sharding import Mesh, PartitionSpec as P

beta_one = 0.9
beta_two = 0.999
adam_eps = 1e-08
learn_rate = 0.01
corr_two = 0.6323045752

F32 = jnp.float32
BF16 = jnp.bfloat16
LANES = 128
PARAMS = pltpu.CompilerParams(vmem_limit_bytes=40 * 1024 * 1024)


def dot(a, b, over, precision=None):
    return lax.dot_general(
        a, b, (((over[0],), (over[1],)), ((), ())), precision=precision, preferred_element_type=F32
    )


def expert_base():
    return ((lax.axis_index("ey") * 2 + lax.axis_index("core")) * 2).astype(F32)


def routed(meta, base, tokens, rows):
    count = meta.shape[0]
    meta = meta.astype(F32)
    ids, gates = meta[:, :8], meta[:, 8:16]
    hits = [ids == base + e for e in range(2)]
    named = [jnp.sum(jnp.where(h, 1.0, 0.0), axis=1, keepdims=True) for h in hits]
    gate = [jnp.sum(jnp.where(h, gates, 0.0), axis=1, keepdims=True) for h in hits]
    lane = lax.broadcasted_iota(jnp.int32, (count, LANES), 1)
    marks = jnp.where(lane == 0, named[0], jnp.where(lane == 1, named[1], 0.0)).astype(BF16)
    row_i = lax.broadcasted_iota(jnp.int32, (count, count), 0)
    col_i = lax.broadcasted_iota(jnp.int32, (count, count), 1)
    earlier = ((row_i // tokens == col_i // tokens) & (col_i < row_i)).astype(F32).astype(BF16)
    rank = dot(earlier, marks, (1, 0))
    block = (lax.broadcasted_iota(jnp.int32, (count, 1), 0) // tokens).astype(F32)
    slot_rows = (count // tokens) * rows
    slot_lane = lax.broadcasted_iota(jnp.int32, (count, slot_rows), 1).astype(F32)
    keys = [
        jnp.where(named[e] > 0.5, block * rows + 2.0 * rank[:, e : e + 1] + e, -1.0)
        for e in range(2)
    ]
    onehot = ((slot_lane == keys[0]) | (slot_lane == keys[1])).astype(F32).astype(BF16)
    return onehot, gate


def by_expert(hid):
    odd = lax.broadcasted_iota(jnp.int32, hid.shape, 0) % 2
    hid = hid.astype(F32)
    return jnp.concatenate(
        [jnp.where(odd == 0, hid, 0.0), jnp.where(odd == 1, hid, 0.0)], axis=1
    ).astype(BF16)


def gate_lanes(gate):
    return jnp.concatenate([jnp.broadcast_to(g, (g.shape[0], LANES)) for g in gate], axis=1)


def own_kernel(tokens, rows, width, planes, pieces, *refs):
    weight, hid, grad_hidden, gate_part = refs[pieces : pieces + 4]
    grads, toks = refs[pieces + 4 : -1], refs[-1]
    core, line = lax.axis_index("core"), lax.axis_index("ey")
    base = expert_base()
    blocks = grad_hidden.shape[0]
    count = blocks * tokens
    at = 0
    for ref in refs[:pieces]:
        toks[at : at + ref.shape[0], :] = ref[...]
        at += ref.shape[0]
    where = [(line + step) % blocks for step in arrival(blocks)]
    gates_out = None
    scaled = []
    for rel in range(2):
        side = core if rel == 0 else 1 - core
        here = slice(rel * count, (rel + 1) * count)
        onehot, gate = routed(toks[here, width : width + LANES], base, tokens, rows)
        slots = jnp.concatenate([hid[block, side].astype(F32) for block in where], axis=0)
        saved = dot(onehot, by_expert(slots), (1, 0))
        up = dot(toks[here, :width], weight[...], (1, 1))
        scale = gate_lanes(gate)
        scaled.append((scale * saved).astype(BF16))
        picked = dot(onehot, (scale * up).astype(BF16), (0, 0))
        even = lax.broadcasted_iota(jnp.int32, (blocks * rows, LANES), 0) % 2 == 0
        picked = jnp.where(even, picked[:, :LANES], picked[:, LANES:])
        for order, block in enumerate(where):
            grad_hidden[block, side] = picked[order * rows : (order + 1) * rows].astype(BF16)
        prod = saved * up
        lane = lax.broadcasted_iota(jnp.int32, (count, LANES), 1)
        tok = lax.broadcasted_iota(jnp.int32, (count, LANES), 0) % tokens
        spread = jnp.zeros((count, LANES), F32)
        for e in range(2):
            total = jnp.sum(prod[:, e * LANES : (e + 1) * LANES], axis=1, keepdims=True)
            spread = jnp.where(lane == e * tokens + tok, total, spread)
        order = lax.broadcasted_iota(jnp.int32, (2 * blocks, count), 1) // tokens
        away = jnp.where(order % 2 == 1, -((order + 1) // 2), order // 2)
        row = lax.broadcasted_iota(jnp.int32, (2 * blocks, count), 0)
        pick = ((line + away + blocks) % blocks * 2 + side == row).astype(F32)
        piece = dot(pick, spread, (1, 0), lax.Precision.HIGHEST)
        gates_out = piece if gates_out is None else gates_out + piece
    for group in range(2 * blocks):
        values = gates_out[group : group + 1, : 2 * tokens]
        for plane in range(planes):
            gate_part[group * planes + plane] = values
    scaled = jnp.concatenate(scaled, axis=0)
    part = grads[0].shape[0]
    replicas = len(grads)
    for step, grad in enumerate(grads):
        owner = (lax.axis_index("edata") + step) % replicas
        columns = toks[:, pl.ds(pl.multiple_of(owner * part, LANES), part)]
        grad[...] = dot(columns, scaled, (0, 0)).astype(BF16)


def arrival(blocks):
    steps = [0]
    for away in range(1, blocks // 2):
        steps += [blocks - away, away]
    return steps + [blocks // 2]


def home_kernel(tokens, planes, arrived, ids, out):
    groups = arrived.shape[0] // planes
    total = jnp.zeros(ids.shape, F32)
    named = ids[...]
    for group in range(groups):
        line = arrived[group * planes]
        for plane in range(1, planes):
            line = line + arrived[group * planes + plane]
        for e in range(2):
            value = line[:, e * tokens : (e + 1) * tokens]
            total = jnp.where(named == group * 2 + e, value, total)
    out[...] = total


def adam_kernel(part, replicas, *refs):
    weight, one, two, new_weight, new_one, new_two, grad_rows, weight_rows = refs[replicas:]
    total = sum(ref[...].astype(F32) for ref in refs[1:replicas]) + refs[0][...].astype(F32)
    column = pl.multiple_of(lax.axis_index("edata") * part, LANES)
    for e in range(2):
        grad_rows[pl.ds(e, part, 2), :] = total[:, e * LANES : (e + 1) * LANES]
        piece = weight[e * LANES : (e + 1) * LANES, pl.ds(column, part)].astype(F32)
        weight_rows[pl.ds(e, part, 2), :] = piece.T
    g = grad_rows[...]
    first = beta_one * one[...].astype(F32) + (1.0 - beta_one) * g
    second = beta_two * two[...] + (1.0 - beta_two) * g * g
    update = first / (jnp.sqrt(second / corr_two) + adam_eps)
    new_weight[...] = (weight_rows[...] - learn_rate * update).astype(BF16)
    new_one[...] = first.astype(BF16)
    new_two[...] = second


def cost(tokens, terms, moved):
    return pl.CostEstimate(flops=2 * tokens * terms, bytes_accessed=moved, transcendentals=0)


def gathered(own):
    size, half = lax.axis_size("ey"), own.shape[0] // 2
    ahead = [(i, (i + 1) % size) for i in range(size)]
    back = [(i, (i - 1) % size) for i in range(size)]
    swap = [(0, 1), (1, 0)]
    mine = [own]
    up = down = own
    for _ in range(1, size // 2):
        up, down = lax.ppermute(up, "ey", ahead), lax.ppermute(down, "ey", back)
        mine += [up, down]
    last = [lax.ppermute(up[:half], "ey", ahead), lax.ppermute(down[half:], "ey", back)]
    theirs = [lax.ppermute(jnp.concatenate(g, axis=0), "core", swap) for g in (mine, last)]
    return mine + last + theirs


def shards(grad_out, gates, expert_ids, hidden, down_weight, moment_one, moment_two):
    tokens, width = grad_out.shape
    choices = gates.shape[1]
    replicas, planes = lax.axis_size("edata"), lax.axis_size("tensor")
    groups = lax.axis_size("ey") * 2
    held, capacity = hidden.shape[2], hidden.shape[3]
    rows = held * capacity
    part = width // replicas
    every = groups * tokens

    meta = jnp.concatenate(
        [expert_ids.astype(BF16), gates, jnp.zeros((tokens, LANES - 2 * choices), BF16)], axis=1
    )
    toks = gathered(jnp.concatenate([grad_out, meta], axis=1))
    saved = jnp.transpose(hidden[0], (0, 2, 1, 3)).reshape(groups // 2, 2, rows, LANES)
    weight = down_weight.reshape(held * LANES, width)
    grad_hidden, gate_part, *grads = pl.pallas_call(
        functools.partial(own_kernel, tokens, rows, width, planes, len(toks)),
        out_shape=(
            jax.ShapeDtypeStruct(saved.shape, BF16),
            jax.ShapeDtypeStruct((groups * planes, 1, held * tokens), F32),
        )
        + (jax.ShapeDtypeStruct((part, held * LANES), BF16),) * replicas,
        scratch_shapes=[pltpu.VMEM((every, width + LANES), BF16)],
        compiler_params=PARAMS,
        cost_estimate=cost(every, 2 * width * held * LANES, 8 << 20),
        name="own_tokens",
    )(*toks, weight, saved)

    for step in range(1, replicas):
        to_owner = [(i, (i + step) % replicas) for i in range(replicas)]
        grads[step] = lax.ppermute(grads[step], "edata", to_owner)
    gate_home = lax.all_to_all(gate_part, ("ey", "core", "tensor"), 0, 0, tiled=True)
    grad_gates = pl.pallas_call(
        functools.partial(home_kernel, tokens, planes),
        out_shape=jax.ShapeDtypeStruct((choices, tokens), F32),
        compiler_params=PARAMS,
        name="gates_home",
    )(gate_home, expert_ids.T).T

    flat = (part * held, LANES)
    new_weight, new_one, new_two = pl.pallas_call(
        functools.partial(adam_kernel, part, replicas),
        out_shape=(
            jax.ShapeDtypeStruct(flat, BF16),
            jax.ShapeDtypeStruct(flat, BF16),
            jax.ShapeDtypeStruct(flat, F32),
        ),
        scratch_shapes=[pltpu.VMEM(flat, F32), pltpu.VMEM(flat, F32)],
        compiler_params=PARAMS,
        cost_estimate=cost(part, held * LANES, 8 << 20),
        name="adam",
    )(*grads, weight, moment_one.reshape(flat), moment_two.reshape(flat))
    grad_hidden = jnp.transpose(
        grad_hidden.reshape(1, groups, capacity, held, LANES), (0, 1, 3, 2, 4)
    )
    shape = moment_one.shape
    return (
        grad_hidden, grad_gates, new_weight.reshape(shape), new_one.reshape(shape),
        new_two.reshape(shape),
    )


def solution(mesh):
    replicas, groups, planes = mesh.devices.shape
    fine = Mesh(
        mesh.devices.reshape(replicas, groups // 2, 2, planes), ("edata", "ey", "core", "tensor")
    )
    expert = ("ey", "core")
    block = P(("edata", "ey", "core"), None)
    state = P("edata", expert, "tensor")
    saved = P("edata", None, expert, None, "tensor")
    return jax.shard_map(
        shards,
        mesh=fine,
        in_specs=(block, block, block, saved, P(expert, "tensor", None), state, state),
        out_specs=(saved, block, state, state, state),
        check_vma=False,
    )
```

```python
import functools

import jax
import jax.numpy as jnp
from jax import lax
from jax.experimental import pallas as pl
from jax.experimental.pallas import tpu as pltpu
from jax.sharding import Mesh, PartitionSpec as P

beta_one = 0.9
beta_two = 0.999
adam_eps = 1e-08
learn_rate = 0.01
corr_two = 0.6323045752

F32 = jnp.float32
BF16 = jnp.bfloat16
LANES = 128
PARAMS = pltpu.CompilerParams(vmem_limit_bytes=40 * 1024 * 1024)


def dot(a, b, over, precision=None):
    return lax.dot_general(
        a, b, (((over[0],), (over[1],)), ((), ())), precision=precision, preferred_element_type=F32
    )


def expert_base():
    return ((lax.axis_index("ey") * 2 + lax.axis_index("core")) * 2).astype(F32)


def routed(meta, base, tokens, rows):
    count = meta.shape[0]
    meta = meta.astype(F32)
    ids, gates = meta[:, :8], meta[:, 8:16]
    hits = [ids == base + e for e in range(2)]
    named = [jnp.sum(jnp.where(h, 1.0, 0.0), axis=1, keepdims=True) for h in hits]
    gate = [jnp.sum(jnp.where(h, gates, 0.0), axis=1, keepdims=True) for h in hits]
    lane = lax.broadcasted_iota(jnp.int32, (count, LANES), 1)
    marks = jnp.where(lane == 0, named[0], jnp.where(lane == 1, named[1], 0.0)).astype(BF16)
    row_i = lax.broadcasted_iota(jnp.int32, (count, count), 0)
    col_i = lax.broadcasted_iota(jnp.int32, (count, count), 1)
    earlier = ((row_i // tokens == col_i // tokens) & (col_i < row_i)).astype(F32).astype(BF16)
    rank = dot(earlier, marks, (1, 0))
    block = (lax.broadcasted_iota(jnp.int32, (count, 1), 0) // tokens).astype(F32)
    slot_rows = (count // tokens) * rows
    slot_lane = lax.broadcasted_iota(jnp.int32, (count, slot_rows), 1).astype(F32)
    keys = [
        jnp.where(named[e] > 0.5, block * rows + 2.0 * rank[:, e : e + 1] + e, -1.0)
        for e in range(2)
    ]
    onehot = ((slot_lane == keys[0]) | (slot_lane == keys[1])).astype(F32).astype(BF16)
    return onehot, gate


def by_expert(hid):
    odd = lax.broadcasted_iota(jnp.int32, hid.shape, 0) % 2
    hid = hid.astype(F32)
    return jnp.concatenate(
        [jnp.where(odd == 0, hid, 0.0), jnp.where(odd == 1, hid, 0.0)], axis=1
    ).astype(BF16)


def gate_lanes(gate):
    return jnp.concatenate([jnp.broadcast_to(g, (g.shape[0], LANES)) for g in gate], axis=1)


def own_kernel(tokens, rows, width, planes, pieces, *refs):
    weight, hid, grad_hidden, gate_part = refs[pieces : pieces + 4]
    grads, toks = refs[pieces + 4 : -1], refs[-1]
    core, line = lax.axis_index("core"), lax.axis_index("ey")
    base = expert_base()
    blocks = grad_hidden.shape[0]
    count = blocks * tokens
    at = 0
    for ref in refs[:pieces]:
        toks[at : at + ref.shape[0], :] = ref[...]
        at += ref.shape[0]
    where = [(line + step) % blocks for step in arrival(blocks)]
    gates_out = None
    scaled = []
    for rel in range(2):
        side = core if rel == 0 else 1 - core
        here = slice(rel * count, (rel + 1) * count)
        onehot, gate = routed(toks[here, width : width + LANES], base, tokens, rows)
        slots = jnp.concatenate([hid[block, side].astype(F32) for block in where], axis=0)
        saved = dot(onehot, by_expert(slots), (1, 0))
        up = dot(toks[here, :width], weight[...], (1, 1))
        scale = gate_lanes(gate)
        scaled.append((scale * saved).astype(BF16))
        picked = dot(onehot, (scale * up).astype(BF16), (0, 0))
        even = lax.broadcasted_iota(jnp.int32, (blocks * rows, LANES), 0) % 2 == 0
        picked = jnp.where(even, picked[:, :LANES], picked[:, LANES:])
        for order, block in enumerate(where):
            grad_hidden[block, side] = picked[order * rows : (order + 1) * rows].astype(BF16)
        prod = saved * up
        lane = lax.broadcasted_iota(jnp.int32, (count, LANES), 1)
        tok = lax.broadcasted_iota(jnp.int32, (count, LANES), 0) % tokens
        spread = jnp.zeros((count, LANES), F32)
        for e in range(2):
            total = jnp.sum(prod[:, e * LANES : (e + 1) * LANES], axis=1, keepdims=True)
            spread = jnp.where(lane == e * tokens + tok, total, spread)
        order = lax.broadcasted_iota(jnp.int32, (2 * blocks, count), 1) // tokens
        away = jnp.zeros_like(order)
        for place, step in enumerate(arrival(blocks)):
            away = jnp.where(order == place, step, away)
        row = lax.broadcasted_iota(jnp.int32, (2 * blocks, count), 0)
        pick = ((line + away) % blocks * 2 + side == row).astype(F32)
        piece = dot(pick, spread, (1, 0), lax.Precision.HIGHEST)
        gates_out = piece if gates_out is None else gates_out + piece
    for group in range(2 * blocks):
        values = gates_out[group : group + 1, : 2 * tokens]
        for plane in range(planes):
            gate_part[group * planes + plane] = values
    scaled = jnp.concatenate(scaled, axis=0)
    part = grads[0].shape[0]
    replicas = len(grads)
    for step, grad in enumerate(grads):
        owner = (lax.axis_index("edata") + step) % replicas
        columns = toks[:, pl.ds(pl.multiple_of(owner * part, LANES), part)]
        grad[...] = dot(columns, scaled, (0, 0)).astype(BF16)


def arrival(blocks):
    steps = [0]
    for away in range(1, blocks // 2):
        steps += [blocks - away, away]
    return steps[:-2] + [blocks // 2] + steps[-2:]


def home_kernel(tokens, planes, arrived, ids, out):
    groups = arrived.shape[0] // planes
    total = jnp.zeros(ids.shape, F32)
    named = ids[...]
    for group in range(groups):
        line = arrived[group * planes]
        for plane in range(1, planes):
            line = line + arrived[group * planes + plane]
        for e in range(2):
            value = line[:, e * tokens : (e + 1) * tokens]
            total = jnp.where(named == group * 2 + e, value, total)
    out[...] = total


def adam_kernel(part, replicas, *refs):
    weight, one, two, new_weight, new_one, new_two, grad_rows, weight_rows = refs[replicas:]
    total = sum(ref[...].astype(F32) for ref in refs[1:replicas]) + refs[0][...].astype(F32)
    column = pl.multiple_of(lax.axis_index("edata") * part, LANES)
    for e in range(2):
        grad_rows[pl.ds(e, part, 2), :] = total[:, e * LANES : (e + 1) * LANES]
        piece = weight[e * LANES : (e + 1) * LANES, pl.ds(column, part)].astype(F32)
        weight_rows[pl.ds(e, part, 2), :] = piece.T
    g = grad_rows[...]
    first = beta_one * one[...].astype(F32) + (1.0 - beta_one) * g
    second = beta_two * two[...] + (1.0 - beta_two) * g * g
    update = first / (jnp.sqrt(second / corr_two) + adam_eps)
    new_weight[...] = (weight_rows[...] - learn_rate * update).astype(BF16)
    new_one[...] = first.astype(BF16)
    new_two[...] = second


def cost(tokens, terms, moved):
    return pl.CostEstimate(flops=2 * tokens * terms, bytes_accessed=moved, transcendentals=0)


def gathered(own):
    size = lax.axis_size("ey")

    def turn(block, by):
        return lax.ppermute(block, "ey", [(i, (i + by) % size) for i in range(size)])

    up, down = turn(own, 1), turn(own, -1)
    far = turn(own, size // 2)
    mine = [own, up, down]
    for _ in range(2, size // 2 - 1):
        up, down = turn(up, 1), turn(down, -1)
        mine += [up, down]
    last = [far, turn(up, 1), turn(down, -1)]
    swap = [(0, 1), (1, 0)]
    theirs = [lax.ppermute(jnp.concatenate(g, axis=0), "core", swap) for g in (mine, last)]
    return mine + last + theirs


def shards(grad_out, gates, expert_ids, hidden, down_weight, moment_one, moment_two):
    tokens, width = grad_out.shape
    choices = gates.shape[1]
    replicas, planes = lax.axis_size("edata"), lax.axis_size("tensor")
    groups = lax.axis_size("ey") * 2
    held, capacity = hidden.shape[2], hidden.shape[3]
    rows = held * capacity
    part = width // replicas
    every = groups * tokens

    meta = jnp.concatenate(
        [expert_ids.astype(BF16), gates, jnp.zeros((tokens, LANES - 2 * choices), BF16)], axis=1
    )
    toks = gathered(jnp.concatenate([grad_out, meta], axis=1))
    saved = jnp.transpose(hidden[0], (0, 2, 1, 3)).reshape(groups // 2, 2, rows, LANES)
    weight = down_weight.reshape(held * LANES, width)
    grad_hidden, gate_part, *grads = pl.pallas_call(
        functools.partial(own_kernel, tokens, rows, width, planes, len(toks)),
        out_shape=(
            jax.ShapeDtypeStruct(saved.shape, BF16),
            jax.ShapeDtypeStruct((groups * planes, 1, held * tokens), F32),
        )
        + (jax.ShapeDtypeStruct((part, held * LANES), BF16),) * replicas,
        scratch_shapes=[pltpu.VMEM((every, width + LANES), BF16)],
        compiler_params=PARAMS,
        cost_estimate=cost(every, 2 * width * held * LANES, 8 << 20),
        name="own_tokens",
    )(*toks, weight, saved)

    for step in range(1, replicas):
        to_owner = [(i, (i + step) % replicas) for i in range(replicas)]
        grads[step] = lax.ppermute(grads[step], "edata", to_owner)
    gate_home = lax.all_to_all(gate_part, ("ey", "core", "tensor"), 0, 0, tiled=True)
    grad_gates = pl.pallas_call(
        functools.partial(home_kernel, tokens, planes),
        out_shape=jax.ShapeDtypeStruct((choices, tokens), F32),
        compiler_params=PARAMS,
        name="gates_home",
    )(gate_home, expert_ids.T).T

    flat = (part * held, LANES)
    new_weight, new_one, new_two = pl.pallas_call(
        functools.partial(adam_kernel, part, replicas),
        out_shape=(
            jax.ShapeDtypeStruct(flat, BF16),
            jax.ShapeDtypeStruct(flat, BF16),
            jax.ShapeDtypeStruct(flat, F32),
        ),
        scratch_shapes=[pltpu.VMEM(flat, F32), pltpu.VMEM(flat, F32)],
        compiler_params=PARAMS,
        cost_estimate=cost(part, held * LANES, 8 << 20),
        name="adam",
    )(*grads, weight, moment_one.reshape(flat), moment_two.reshape(flat))
    grad_hidden = jnp.transpose(
        grad_hidden.reshape(1, groups, capacity, held, LANES), (0, 1, 3, 2, 4)
    )
    shape = moment_one.shape
    return (
        grad_hidden, grad_gates, new_weight.reshape(shape), new_one.reshape(shape),
        new_two.reshape(shape),
    )


def solution(mesh):
    replicas, groups, planes = mesh.devices.shape
    fine = Mesh(
        mesh.devices.reshape(replicas, groups // 2, 2, planes), ("edata", "ey", "core", "tensor")
    )
    expert = ("ey", "core")
    block = P(("edata", "ey", "core"), None)
    state = P("edata", expert, "tensor")
    saved = P("edata", None, expert, None, "tensor")
    return jax.shard_map(
        shards,
        mesh=fine,
        in_specs=(block, block, block, saved, P(expert, "tensor", None), state, state),
        out_specs=(saved, block, state, state, state),
        check_vma=False,
    )
```

```python
import functools

import jax
import jax.numpy as jnp
from jax import lax
from jax.experimental import pallas as pl
from jax.experimental.pallas import tpu as pltpu
from jax.sharding import Mesh, PartitionSpec as P

beta_one = 0.9
beta_two = 0.999
adam_eps = 1e-08
learn_rate = 0.01
corr_two = 0.6323045752

F32 = jnp.float32
BF16 = jnp.bfloat16
LANES = 128
PARAMS = pltpu.CompilerParams(vmem_limit_bytes=24 * 1024 * 1024)


def dot(a, b, over, precision=None):
    return lax.dot_general(
        a, b, (((over[0],), (over[1],)), ((), ())), precision=precision, preferred_element_type=F32
    )


def expert_base():
    return ((lax.axis_index("ey") * 2 + lax.axis_index("core")) * 2).astype(F32)


def routed(meta, base, tokens, rows):
    count = meta.shape[0]
    meta = meta.astype(F32)
    ids, gates = meta[:, :8], meta[:, 8:16]
    hits = [ids == base + e for e in range(2)]
    named = [jnp.sum(jnp.where(h, 1.0, 0.0), axis=1, keepdims=True) for h in hits]
    gate = [jnp.sum(jnp.where(h, gates, 0.0), axis=1, keepdims=True) for h in hits]
    lane = lax.broadcasted_iota(jnp.int32, (count, LANES), 1)
    marks = jnp.where(lane == 0, named[0], jnp.where(lane == 1, named[1], 0.0)).astype(BF16)
    row_i = lax.broadcasted_iota(jnp.int32, (count, count), 0)
    col_i = lax.broadcasted_iota(jnp.int32, (count, count), 1)
    earlier = ((row_i // tokens == col_i // tokens) & (col_i < row_i)).astype(F32).astype(BF16)
    rank = dot(earlier, marks, (1, 0))
    block = (lax.broadcasted_iota(jnp.int32, (count, 1), 0) // tokens).astype(F32)
    slot_rows = (count // tokens) * rows
    slot_lane = lax.broadcasted_iota(jnp.int32, (count, slot_rows), 1).astype(F32)
    keys = [
        jnp.where(named[e] > 0.5, block * rows + 2.0 * rank[:, e : e + 1] + e, -1.0)
        for e in range(2)
    ]
    onehot = ((slot_lane == keys[0]) | (slot_lane == keys[1])).astype(F32).astype(BF16)
    return onehot, gate


def by_expert(hid):
    odd = lax.broadcasted_iota(jnp.int32, hid.shape, 0) % 2
    hid = hid.astype(F32)
    return jnp.concatenate(
        [jnp.where(odd == 0, hid, 0.0), jnp.where(odd == 1, hid, 0.0)], axis=1
    ).astype(BF16)


def gate_lanes(gate):
    return jnp.concatenate([jnp.broadcast_to(g, (g.shape[0], LANES)) for g in gate], axis=1)


def pack_kernel(rows_in, ids, gates, out):
    width, tokens = rows_in.shape[1], rows_in.shape[0]
    out[:, :width] = rows_in[...]
    turned = jnp.concatenate([ids[...].astype(F32), gates[...].astype(F32)], axis=0)
    turned = jnp.concatenate([turned, jnp.zeros((turned.shape[0], LANES - tokens), F32)], axis=1)
    turned = jnp.concatenate([turned, jnp.zeros((tokens - turned.shape[0], LANES), F32)], axis=0)
    out[:, width:] = turned.astype(BF16)


def by_token(meta, tokens):
    meta = meta.astype(F32)
    blocks = [meta[at : at + tokens, :].T for at in range(0, meta.shape[0], tokens)]
    return jnp.concatenate([block[:tokens, :] for block in blocks], axis=0)


def own_kernel(tokens, rows, width, planes, pieces, *refs):
    weight, hid, grad_hidden, gate_part = refs[pieces : pieces + 4]
    grads, toks = refs[pieces + 4 : -1], refs[-1]
    core, line = lax.axis_index("core"), lax.axis_index("ey")
    base = expert_base()
    blocks = grad_hidden.shape[0]
    count = blocks * tokens
    at = 0
    for ref in refs[:pieces]:
        toks[at : at + ref.shape[0], :] = ref[...]
        at += ref.shape[0]
    where = [(line + step) % blocks for step in arrival(blocks)]
    gates_out = None
    scaled = []
    for rel in range(2):
        side = core if rel == 0 else 1 - core
        here = slice(rel * count, (rel + 1) * count)
        onehot, gate = routed(by_token(toks[here, width : width + LANES], tokens), base, tokens, rows)
        slots = jnp.concatenate([hid[block, side].astype(F32) for block in where], axis=0)
        saved = dot(onehot, by_expert(slots), (1, 0))
        up = dot(toks[here, :width], weight[...], (1, 1))
        scale = gate_lanes(gate)
        scaled.append((scale * saved).astype(BF16))
        picked = dot(onehot, (scale * up).astype(BF16), (0, 0))
        even = lax.broadcasted_iota(jnp.int32, (blocks * rows, LANES), 0) % 2 == 0
        picked = jnp.where(even, picked[:, :LANES], picked[:, LANES:])
        for order, block in enumerate(where):
            grad_hidden[block, side] = picked[order * rows : (order + 1) * rows].astype(BF16)
        prod = saved * up
        lane = lax.broadcasted_iota(jnp.int32, (count, LANES), 1)
        tok = lax.broadcasted_iota(jnp.int32, (count, LANES), 0) % tokens
        spread = jnp.zeros((count, LANES), F32)
        for e in range(2):
            total = jnp.sum(prod[:, e * LANES : (e + 1) * LANES], axis=1, keepdims=True)
            spread = jnp.where(lane == e * tokens + tok, total, spread)
        order = lax.broadcasted_iota(jnp.int32, (2 * blocks, count), 1) // tokens
        away = jnp.zeros_like(order)
        for place, step in enumerate(arrival(blocks)):
            away = jnp.where(order == place, step, away)
        row = lax.broadcasted_iota(jnp.int32, (2 * blocks, count), 0)
        pick = ((line + away) % blocks * 2 + side == row).astype(F32)
        piece = dot(pick, spread, (1, 0), lax.Precision.HIGHEST)
        gates_out = piece if gates_out is None else gates_out + piece
    for group in range(2 * blocks):
        values = gates_out[group : group + 1, : 2 * tokens]
        for plane in range(planes):
            gate_part[group * planes + plane] = values
    scaled = jnp.concatenate(scaled, axis=0)
    part = grads[0].shape[0]
    replicas = len(grads)
    for step, grad in enumerate(grads):
        owner = (lax.axis_index("edata") + step) % replicas
        columns = toks[:, pl.ds(pl.multiple_of(owner * part, LANES), part)]
        grad[...] = dot(columns, scaled, (0, 0)).astype(BF16)


def arrival(blocks):
    steps = [0]
    for away in range(1, blocks // 2):
        steps += [blocks - away, away]
    return steps[:-2] + [blocks // 2] + steps[-2:]


def home_kernel(tokens, planes, arrived, ids, out):
    groups = arrived.shape[0] // planes
    total = jnp.zeros(ids.shape, F32)
    named = ids[...]
    for group in range(groups):
        line = arrived[group * planes]
        for plane in range(1, planes):
            line = line + arrived[group * planes + plane]
        for e in range(2):
            value = line[:, e * tokens : (e + 1) * tokens]
            total = jnp.where(named == group * 2 + e, value, total)
    out[...] = total


def adam_kernel(part, replicas, *refs):
    weight, one, two, new_weight, new_one, new_two, grad_rows, weight_rows = refs[replicas:]
    total = sum(ref[...].astype(F32) for ref in refs[1:replicas]) + refs[0][...].astype(F32)
    column = pl.multiple_of(lax.axis_index("edata") * part, LANES)
    for e in range(2):
        grad_rows[pl.ds(e, part, 2), :] = total[:, e * LANES : (e + 1) * LANES]
        piece = weight[e * LANES : (e + 1) * LANES, pl.ds(column, part)].astype(F32)
        weight_rows[pl.ds(e, part, 2), :] = piece.T
    g = grad_rows[...]
    first = beta_one * one[...].astype(F32) + (1.0 - beta_one) * g
    second = beta_two * two[...] + (1.0 - beta_two) * g * g
    update = first / (jnp.sqrt(second / corr_two) + adam_eps)
    new_weight[...] = (weight_rows[...] - learn_rate * update).astype(BF16)
    new_one[...] = first.astype(BF16)
    new_two[...] = second


def cost(tokens, terms, moved):
    return pl.CostEstimate(flops=2 * tokens * terms, bytes_accessed=moved, transcendentals=0)


def gathered(own):
    size = lax.axis_size("ey")

    def turn(block, by):
        return lax.ppermute(block, "ey", [(i, (i + by) % size) for i in range(size)])

    up, down = turn(own, 1), turn(own, -1)
    mine = [own, up, down]
    for _ in range(2, size // 2 - 1):
        up, down = turn(up, 1), turn(down, -1)
        mine += [up, down]
    again, up, down = lax.optimization_barrier((own, up, down))
    far = turn(again, size // 2)
    mine[-2:] = [up, down]
    last = [far, turn(up, 1), turn(down, -1)]
    swap = [(0, 1), (1, 0)]
    theirs = [lax.ppermute(jnp.concatenate(g, axis=0), "core", swap) for g in (mine, last)]
    return mine + last + theirs


def shards(grad_out, gates, expert_ids, hidden, down_weight, moment_one, moment_two):
    tokens, width = grad_out.shape
    choices = gates.shape[1]
    replicas, planes = lax.axis_size("edata"), lax.axis_size("tensor")
    groups = lax.axis_size("ey") * 2
    held, capacity = hidden.shape[2], hidden.shape[3]
    rows = held * capacity
    part = width // replicas
    every = groups * tokens

    toks = gathered(
        pl.pallas_call(
            pack_kernel,
            out_shape=jax.ShapeDtypeStruct((tokens, width + LANES), BF16),
            compiler_params=PARAMS,
            name="pack",
        )(grad_out, expert_ids.T, gates.T)
    )
    saved = jnp.transpose(hidden[0], (0, 2, 1, 3)).reshape(groups // 2, 2, rows, LANES)
    weight = down_weight.reshape(held * LANES, width)
    grad_hidden, gate_part, *grads = pl.pallas_call(
        functools.partial(own_kernel, tokens, rows, width, planes, len(toks)),
        out_shape=(
            jax.ShapeDtypeStruct(saved.shape, BF16),
            jax.ShapeDtypeStruct((groups * planes, 1, held * tokens), F32),
        )
        + (jax.ShapeDtypeStruct((part, held * LANES), BF16),) * replicas,
        scratch_shapes=[pltpu.VMEM((every, width + LANES), BF16)],
        compiler_params=PARAMS,
        cost_estimate=cost(every, 2 * width * held * LANES, 8 << 20),
        name="own_tokens",
    )(*toks, weight, saved)

    for step in range(1, replicas):
        to_owner = [(i, (i + step) % replicas) for i in range(replicas)]
        grads[step] = lax.ppermute(grads[step], "edata", to_owner)
    gate_home = lax.all_to_all(gate_part, ("ey", "core", "tensor"), 0, 0, tiled=True)
    flat = (part * held, LANES)
    new_weight, new_one, new_two = pl.pallas_call(
        functools.partial(adam_kernel, part, replicas),
        out_shape=(
            jax.ShapeDtypeStruct(flat, BF16),
            jax.ShapeDtypeStruct(flat, BF16),
            jax.ShapeDtypeStruct(flat, F32),
        ),
        scratch_shapes=[pltpu.VMEM(flat, F32), pltpu.VMEM(flat, F32)],
        compiler_params=PARAMS,
        cost_estimate=cost(part, held * LANES, 8 << 20),
        name="adam",
    )(*grads, weight, moment_one.reshape(flat), moment_two.reshape(flat))
    gate_home, new_one = lax.optimization_barrier((gate_home, new_one))
    grad_gates = pl.pallas_call(
        functools.partial(home_kernel, tokens, planes),
        out_shape=jax.ShapeDtypeStruct((choices, tokens), F32),
        compiler_params=PARAMS,
        name="gates_home",
    )(gate_home, expert_ids.T).T
    grad_hidden = jnp.transpose(
        grad_hidden.reshape(1, groups, capacity, held, LANES), (0, 1, 3, 2, 4)
    )
    shape = moment_one.shape
    return (
        grad_hidden, grad_gates, new_weight.reshape(shape), new_one.reshape(shape),
        new_two.reshape(shape),
    )


def solution(mesh):
    replicas, groups, planes = mesh.devices.shape
    fine = Mesh(
        mesh.devices.reshape(replicas, groups // 2, 2, planes), ("edata", "ey", "core", "tensor")
    )
    expert = ("ey", "core")
    block = P(("edata", "ey", "core"), None)
    state = P("edata", expert, "tensor")
    saved = P("edata", None, expert, None, "tensor")
    return jax.shard_map(
        shards,
        mesh=fine,
        in_specs=(block, block, block, saved, P(expert, "tensor", None), state, state),
        out_specs=(saved, block, state, state, state),
        check_vma=False,
    )
```

```python
import functools

import jax
import jax.numpy as jnp
from jax import lax
from jax.experimental import pallas as pl
from jax.experimental.pallas import tpu as pltpu
from jax.sharding import Mesh, PartitionSpec as P

beta_one = 0.9
beta_two = 0.999
adam_eps = 1e-08
learn_rate = 0.01
corr_two = 0.6323045752

F32 = jnp.float32
BF16 = jnp.bfloat16
LANES = 128
PARAMS = pltpu.CompilerParams(vmem_limit_bytes=24 * 1024 * 1024)


def dot(a, b, over, precision=None):
    return lax.dot_general(
        a, b, (((over[0],), (over[1],)), ((), ())), precision=precision, preferred_element_type=F32
    )


def expert_base():
    return ((lax.axis_index("ey") * 2 + lax.axis_index("core")) * 2).astype(F32)


def routed(meta, base, tokens, rows):
    count = meta.shape[0]
    meta = meta.astype(F32)
    ids, gates = meta[:, :8], meta[:, 8:16]
    hits = [ids == base + e for e in range(2)]
    named = [jnp.sum(jnp.where(h, 1.0, 0.0), axis=1, keepdims=True) for h in hits]
    gate = [jnp.sum(jnp.where(h, gates, 0.0), axis=1, keepdims=True) for h in hits]
    lane = lax.broadcasted_iota(jnp.int32, (count, LANES), 1)
    marks = jnp.where(lane == 0, named[0], jnp.where(lane == 1, named[1], 0.0)).astype(BF16)
    row_i = lax.broadcasted_iota(jnp.int32, (count, count), 0)
    col_i = lax.broadcasted_iota(jnp.int32, (count, count), 1)
    earlier = ((row_i // tokens == col_i // tokens) & (col_i < row_i)).astype(F32).astype(BF16)
    rank = dot(earlier, marks, (1, 0))
    block = (lax.broadcasted_iota(jnp.int32, (count, 1), 0) // tokens).astype(F32)
    slot_rows = (count // tokens) * rows
    slot_lane = lax.broadcasted_iota(jnp.int32, (count, slot_rows), 1).astype(F32)
    keys = [
        jnp.where(named[e] > 0.5, block * rows + 2.0 * rank[:, e : e + 1] + e, -1.0)
        for e in range(2)
    ]
    onehot = ((slot_lane == keys[0]) | (slot_lane == keys[1])).astype(F32).astype(BF16)
    return onehot, gate


def by_expert(hid):
    odd = lax.broadcasted_iota(jnp.int32, hid.shape, 0) % 2
    hid = hid.astype(F32)
    return jnp.concatenate(
        [jnp.where(odd == 0, hid, 0.0), jnp.where(odd == 1, hid, 0.0)], axis=1
    ).astype(BF16)


def gate_lanes(gate):
    return jnp.concatenate([jnp.broadcast_to(g, (g.shape[0], LANES)) for g in gate], axis=1)


def pack_kernel(rows_in, ids_in, gates_in, out, ids, gates, sems):
    tokens, width = rows_in.shape
    rows_copy = pltpu.make_async_copy(rows_in, out.at[:, pl.ds(0, width)], sems.at[0])
    ids_copy = pltpu.make_async_copy(ids_in, ids, sems.at[1])
    gates_copy = pltpu.make_async_copy(gates_in, gates, sems.at[2])
    rows_copy.start()
    ids_copy.start()
    gates_copy.start()
    ids_copy.wait()
    gates_copy.wait()
    lying = jnp.concatenate([ids[...].astype(F32), gates[...].astype(F32)], axis=0)
    lying = jnp.concatenate([lying, jnp.zeros((lying.shape[0], LANES - tokens), F32)], axis=1)
    lying = jnp.concatenate([lying, jnp.zeros((LANES - lying.shape[0], LANES), F32)], axis=0)
    out[:, width:] = lying.T[:tokens, :].astype(BF16)
    rows_copy.wait()


def own_kernel(tokens, rows, width, planes, pieces, *refs):
    weight, hid, grad_hidden, gate_part = refs[pieces : pieces + 4]
    grads, toks = refs[pieces + 4 : -1], refs[-1]
    core, line = lax.axis_index("core"), lax.axis_index("ey")
    base = expert_base()
    blocks = grad_hidden.shape[0]
    count = blocks * tokens
    at = 0
    for ref in refs[:pieces]:
        toks[at : at + ref.shape[0], :] = ref[...]
        at += ref.shape[0]
    where = [(line + step) % blocks for step in arrival(blocks)]
    gates_out = None
    scaled = []
    for rel in range(2):
        side = core if rel == 0 else 1 - core
        here = slice(rel * count, (rel + 1) * count)
        onehot, gate = routed(toks[here, width : width + LANES], base, tokens, rows)
        slots = jnp.concatenate([hid[block, side].astype(F32) for block in where], axis=0)
        saved = dot(onehot, by_expert(slots), (1, 0))
        up = dot(toks[here, :width], weight[...], (1, 1))
        scale = gate_lanes(gate)
        scaled.append((scale * saved).astype(BF16))
        picked = dot(onehot, (scale * up).astype(BF16), (0, 0))
        even = lax.broadcasted_iota(jnp.int32, (blocks * rows, LANES), 0) % 2 == 0
        picked = jnp.where(even, picked[:, :LANES], picked[:, LANES:])
        for order, block in enumerate(where):
            grad_hidden[block, side] = picked[order * rows : (order + 1) * rows].astype(BF16)
        prod = saved * up
        lane = lax.broadcasted_iota(jnp.int32, (count, LANES), 1)
        tok = lax.broadcasted_iota(jnp.int32, (count, LANES), 0) % tokens
        spread = jnp.zeros((count, LANES), F32)
        for e in range(2):
            total = jnp.sum(prod[:, e * LANES : (e + 1) * LANES], axis=1, keepdims=True)
            spread = jnp.where(lane == e * tokens + tok, total, spread)
        order = lax.broadcasted_iota(jnp.int32, (2 * blocks, count), 1) // tokens
        away = jnp.zeros_like(order)
        for place, step in enumerate(arrival(blocks)):
            away = jnp.where(order == place, step, away)
        row = lax.broadcasted_iota(jnp.int32, (2 * blocks, count), 0)
        pick = ((line + away) % blocks * 2 + side == row).astype(F32)
        piece = dot(pick, spread, (1, 0), lax.Precision.HIGHEST)
        gates_out = piece if gates_out is None else gates_out + piece
    for group in range(2 * blocks):
        values = gates_out[group : group + 1, : 2 * tokens]
        for plane in range(planes):
            gate_part[group * planes + plane] = values
    scaled = jnp.concatenate(scaled, axis=0)
    part = grads[0].shape[0]
    replicas = len(grads)
    for step, grad in enumerate(grads):
        owner = (lax.axis_index("edata") + step) % replicas
        columns = toks[:, pl.ds(pl.multiple_of(owner * part, LANES), part)]
        grad[...] = dot(columns, scaled, (0, 0)).astype(BF16)


def arrival(blocks):
    steps = [0]
    for away in range(1, blocks // 2):
        steps += [blocks - away, away]
    return steps[:-2] + [blocks // 2] + steps[-2:]


def home_kernel(tokens, planes, arrived, ids, out):
    groups = arrived.shape[0] // planes
    total = jnp.zeros(ids.shape, F32)
    named = ids[...]
    for group in range(groups):
        line = arrived[group * planes]
        for plane in range(1, planes):
            line = line + arrived[group * planes + plane]
        for e in range(2):
            value = line[:, e * tokens : (e + 1) * tokens]
            total = jnp.where(named == group * 2 + e, value, total)
    out[...] = total


def adam_kernel(part, replicas, *refs):
    weight, one, two, new_weight, new_one, new_two, grad_rows, weight_rows = refs[replicas:]
    total = sum(ref[...].astype(F32) for ref in refs[1:replicas]) + refs[0][...].astype(F32)
    column = pl.multiple_of(lax.axis_index("edata") * part, LANES)
    for e in range(2):
        grad_rows[pl.ds(e, part, 2), :] = total[:, e * LANES : (e + 1) * LANES]
        piece = weight[e * LANES : (e + 1) * LANES, pl.ds(column, part)].astype(F32)
        weight_rows[pl.ds(e, part, 2), :] = piece.T
    g = grad_rows[...]
    first = beta_one * one[...].astype(F32) + (1.0 - beta_one) * g
    second = beta_two * two[...] + (1.0 - beta_two) * g * g
    update = first / (jnp.sqrt(second / corr_two) + adam_eps)
    new_weight[...] = (weight_rows[...] - learn_rate * update).astype(BF16)
    new_one[...] = first.astype(BF16)
    new_two[...] = second


def cost(tokens, terms, moved):
    return pl.CostEstimate(flops=2 * tokens * terms, bytes_accessed=moved, transcendentals=0)


def gathered(own):
    size = lax.axis_size("ey")

    def turn(block, by):
        return lax.ppermute(block, "ey", [(i, (i + by) % size) for i in range(size)])

    up, down = turn(own, 1), turn(own, -1)
    mine = [own, up, down]
    for _ in range(2, size // 2 - 1):
        up, down = turn(up, 1), turn(down, -1)
        mine += [up, down]
    again, up, down = lax.optimization_barrier((own, up, down))
    far = turn(again, size // 2)
    mine[-2:] = [up, down]
    last = [far, turn(up, 1), turn(down, -1)]
    swap = [(0, 1), (1, 0)]
    theirs = [lax.ppermute(jnp.concatenate(g, axis=0), "core", swap) for g in (mine, last)]
    return mine + last + theirs


def shards(grad_out, gates, expert_ids, hidden, down_weight, moment_one, moment_two):
    tokens, width = grad_out.shape
    choices = gates.shape[1]
    replicas, planes = lax.axis_size("edata"), lax.axis_size("tensor")
    groups = lax.axis_size("ey") * 2
    held, capacity = hidden.shape[2], hidden.shape[3]
    rows = held * capacity
    part = width // replicas
    every = groups * tokens

    toks = gathered(
        pl.pallas_call(
            pack_kernel,
            in_specs=[pl.BlockSpec(memory_space=pltpu.HBM)] * 3,
            out_shape=jax.ShapeDtypeStruct((tokens, width + LANES), BF16),
            scratch_shapes=[
                pltpu.VMEM((choices, tokens), jnp.int32),
                pltpu.VMEM((choices, tokens), BF16),
                pltpu.SemaphoreType.DMA((3,)),
            ],
            compiler_params=pltpu.CompilerParams(vmem_limit_bytes=60 * 1024 * 1024),
            name="pack",
        )(grad_out, expert_ids.T, gates.T)
    )
    saved = jnp.transpose(hidden[0], (0, 2, 1, 3)).reshape(groups // 2, 2, rows, LANES)
    weight = down_weight.reshape(held * LANES, width)
    grad_hidden, gate_part, *grads = pl.pallas_call(
        functools.partial(own_kernel, tokens, rows, width, planes, len(toks)),
        out_shape=(
            jax.ShapeDtypeStruct(saved.shape, BF16),
            jax.ShapeDtypeStruct((groups * planes, 1, held * tokens), F32),
        )
        + (jax.ShapeDtypeStruct((part, held * LANES), BF16),) * replicas,
        scratch_shapes=[pltpu.VMEM((every, width + LANES), BF16)],
        compiler_params=PARAMS,
        cost_estimate=cost(every, 2 * width * held * LANES, 8 << 20),
        name="own_tokens",
    )(*toks, weight, saved)

    for step in range(1, replicas):
        to_owner = [(i, (i + step) % replicas) for i in range(replicas)]
        grads[step] = lax.ppermute(grads[step], "edata", to_owner)
    gate_home = lax.all_to_all(gate_part, ("ey", "core", "tensor"), 0, 0, tiled=True)
    flat = (part * held, LANES)
    new_weight, new_one, new_two = pl.pallas_call(
        functools.partial(adam_kernel, part, replicas),
        out_shape=(
            jax.ShapeDtypeStruct(flat, BF16),
            jax.ShapeDtypeStruct(flat, BF16),
            jax.ShapeDtypeStruct(flat, F32),
        ),
        scratch_shapes=[pltpu.VMEM(flat, F32), pltpu.VMEM(flat, F32)],
        compiler_params=PARAMS,
        cost_estimate=cost(part, held * LANES, 8 << 20),
        name="adam",
    )(*grads, weight, moment_one.reshape(flat), moment_two.reshape(flat))
    grad_gates = pl.pallas_call(
        functools.partial(home_kernel, tokens, planes),
        out_shape=jax.ShapeDtypeStruct((choices, tokens), F32),
        compiler_params=PARAMS,
        name="gates_home",
    )(gate_home, expert_ids.T).T
    grad_hidden = jnp.transpose(
        grad_hidden.reshape(1, groups, capacity, held, LANES), (0, 1, 3, 2, 4)
    )
    shape = moment_one.shape
    return (
        grad_hidden, grad_gates, new_weight.reshape(shape), new_one.reshape(shape),
        new_two.reshape(shape),
    )


def solution(mesh):
    replicas, groups, planes = mesh.devices.shape
    fine = Mesh(
        mesh.devices.reshape(replicas, groups // 2, 2, planes), ("edata", "ey", "core", "tensor")
    )
    expert = ("ey", "core")
    block = P(("edata", "ey", "core"), None)
    state = P("edata", expert, "tensor")
    saved = P("edata", None, expert, None, "tensor")
    return jax.shard_map(
        shards,
        mesh=fine,
        in_specs=(block, block, block, saved, P(expert, "tensor", None), state, state),
        out_specs=(saved, block, state, state, state),
        check_vma=False,
    )
```

```python
import functools

import jax
import jax.numpy as jnp
from jax import lax
from jax.experimental import pallas as pl
from jax.experimental.pallas import tpu as pltpu
from jax.sharding import Mesh, PartitionSpec as P

beta_one = 0.9
beta_two = 0.999
adam_eps = 1e-08
learn_rate = 0.01
corr_two = 0.6323045752

F32 = jnp.float32
BF16 = jnp.bfloat16
LANES = 128
PARAMS = pltpu.CompilerParams(vmem_limit_bytes=24 * 1024 * 1024)


def dot(a, b, over, precision=None):
    return lax.dot_general(
        a, b, (((over[0],), (over[1],)), ((), ())), precision=precision, preferred_element_type=F32
    )


def expert_base():
    return ((lax.axis_index("ey") * 2 + lax.axis_index("core")) * 2).astype(F32)


def routed(meta, base, tokens, rows):
    count = meta.shape[0]
    meta = meta.astype(F32)
    ids, gates = meta[:, :8], meta[:, 8:16]
    hits = [ids == base + e for e in range(2)]
    named = [jnp.sum(jnp.where(h, 1.0, 0.0), axis=1, keepdims=True) for h in hits]
    gate = [jnp.sum(jnp.where(h, gates, 0.0), axis=1, keepdims=True) for h in hits]
    lane = lax.broadcasted_iota(jnp.int32, (count, LANES), 1)
    marks = jnp.where(lane == 0, named[0], jnp.where(lane == 1, named[1], 0.0)).astype(BF16)
    row_i = lax.broadcasted_iota(jnp.int32, (count, count), 0)
    col_i = lax.broadcasted_iota(jnp.int32, (count, count), 1)
    earlier = ((row_i // tokens == col_i // tokens) & (col_i < row_i)).astype(F32).astype(BF16)
    rank = dot(earlier, marks, (1, 0))
    block = (lax.broadcasted_iota(jnp.int32, (count, 1), 0) // tokens).astype(F32)
    slot_rows = (count // tokens) * rows
    slot_lane = lax.broadcasted_iota(jnp.int32, (count, slot_rows), 1).astype(F32)
    keys = [
        jnp.where(named[e] > 0.5, block * rows + 2.0 * rank[:, e : e + 1] + e, -1.0)
        for e in range(2)
    ]
    onehot = ((slot_lane == keys[0]) | (slot_lane == keys[1])).astype(F32).astype(BF16)
    return onehot, gate


def by_expert(hid):
    odd = lax.broadcasted_iota(jnp.int32, hid.shape, 0) % 2
    hid = hid.astype(F32)
    return jnp.concatenate(
        [jnp.where(odd == 0, hid, 0.0), jnp.where(odd == 1, hid, 0.0)], axis=1
    ).astype(BF16)


def gate_lanes(gate):
    return jnp.concatenate([jnp.broadcast_to(g, (g.shape[0], LANES)) for g in gate], axis=1)


def pack_kernel(rows_in, ids_in, gates_in, out, ids, gates, sems):
    tokens, width = rows_in.shape
    rows_copy = pltpu.make_async_copy(rows_in, out.at[:, pl.ds(0, width)], sems.at[0])
    ids_copy = pltpu.make_async_copy(ids_in, ids, sems.at[1])
    gates_copy = pltpu.make_async_copy(gates_in, gates, sems.at[2])
    rows_copy.start()
    ids_copy.start()
    gates_copy.start()
    ids_copy.wait()
    gates_copy.wait()
    lying = jnp.concatenate([ids[...].astype(F32), gates[...].astype(F32)], axis=0)
    lying = jnp.concatenate([lying, jnp.zeros((lying.shape[0], LANES - tokens), F32)], axis=1)
    lying = jnp.concatenate([lying, jnp.zeros((LANES - lying.shape[0], LANES), F32)], axis=0)
    out[:, width:] = lying.T[:tokens, :].astype(BF16)
    rows_copy.wait()


def own_kernel(tokens, rows, width, planes, pieces, *refs):
    weight, hid, grad_hidden, gate_part = refs[pieces : pieces + 4]
    grads, toks = refs[pieces + 4 : -1], refs[-1]
    core, line = lax.axis_index("core"), lax.axis_index("ey")
    base = expert_base()
    blocks = grad_hidden.shape[0]
    count = blocks * tokens
    at = 0
    for ref in refs[:pieces]:
        toks[at : at + ref.shape[0], :] = ref[...]
        at += ref.shape[0]
    where = [(line + step) % blocks for step in arrival(blocks)]
    gates_out = None
    scaled = []
    for rel in range(2):
        side = core if rel == 0 else 1 - core
        here = slice(rel * count, (rel + 1) * count)
        onehot, gate = routed(toks[here, width : width + LANES], base, tokens, rows)
        slots = jnp.concatenate([hid[block, side].astype(F32) for block in where], axis=0)
        saved = dot(onehot, by_expert(slots), (1, 0))
        up = dot(toks[here, :width], weight[...], (1, 1))
        scale = gate_lanes(gate)
        scaled.append((scale * saved).astype(BF16))
        picked = dot(onehot, (scale * up).astype(BF16), (0, 0))
        even = lax.broadcasted_iota(jnp.int32, (blocks * rows, LANES), 0) % 2 == 0
        picked = jnp.where(even, picked[:, :LANES], picked[:, LANES:])
        for order, block in enumerate(where):
            grad_hidden[block, side] = picked[order * rows : (order + 1) * rows].astype(BF16)
        prod = saved * up
        lane = lax.broadcasted_iota(jnp.int32, (count, LANES), 1)
        tok = lax.broadcasted_iota(jnp.int32, (count, LANES), 0) % tokens
        spread = jnp.zeros((count, LANES), F32)
        for e in range(2):
            total = jnp.sum(prod[:, e * LANES : (e + 1) * LANES], axis=1, keepdims=True)
            spread = jnp.where(lane == e * tokens + tok, total, spread)
        order = lax.broadcasted_iota(jnp.int32, (2 * blocks, count), 1) // tokens
        away = jnp.zeros_like(order)
        for place, step in enumerate(arrival(blocks)):
            away = jnp.where(order == place, step, away)
        row = lax.broadcasted_iota(jnp.int32, (2 * blocks, count), 0)
        pick = ((line + away) % blocks * 2 + side == row).astype(F32)
        piece = dot(pick, spread, (1, 0), lax.Precision.HIGHEST)
        gates_out = piece if gates_out is None else gates_out + piece
    for group in range(2 * blocks):
        values = gates_out[group : group + 1, : 2 * tokens]
        for plane in range(planes):
            gate_part[group * planes + plane] = values
    scaled = jnp.concatenate(scaled, axis=0)
    part = grads[0].shape[0]
    replicas = len(grads)
    for step, grad in enumerate(grads):
        owner = (lax.axis_index("edata") + step) % replicas
        columns = toks[:, pl.ds(pl.multiple_of(owner * part, LANES), part)]
        grad[...] = dot(columns, scaled, (0, 0)).astype(BF16)


def arrival(blocks):
    steps = [0]
    for away in range(1, blocks // 2):
        steps += [blocks - away, away]
    return steps[:-2] + [blocks // 2] + steps[-2:]


def home_kernel(tokens, planes, arrived, ids, out):
    groups = arrived.shape[0] // planes
    total = jnp.zeros(ids.shape, F32)
    named = ids[...]
    for group in range(groups):
        line = arrived[group * planes]
        for plane in range(1, planes):
            line = line + arrived[group * planes + plane]
        for e in range(2):
            value = line[:, e * tokens : (e + 1) * tokens]
            total = jnp.where(named == group * 2 + e, value, total)
    out[...] = total


def adam_kernel(part, replicas, *refs):
    weight, one, two, new_weight, new_one, new_two, grad_rows, weight_rows = refs[replicas:]
    total = sum(ref[...].astype(F32) for ref in refs[1:replicas]) + refs[0][...].astype(F32)
    column = pl.multiple_of(lax.axis_index("edata") * part, LANES)
    for e in range(2):
        grad_rows[pl.ds(e, part, 2), :] = total[:, e * LANES : (e + 1) * LANES]
        piece = weight[e * LANES : (e + 1) * LANES, pl.ds(column, part)].astype(F32)
        weight_rows[pl.ds(e, part, 2), :] = piece.T
    g = grad_rows[...]
    first = beta_one * one[...].astype(F32) + (1.0 - beta_one) * g
    second = beta_two * two[...] + (1.0 - beta_two) * g * g
    update = first / (jnp.sqrt(second / corr_two) + adam_eps)
    new_weight[...] = (weight_rows[...] - learn_rate * update).astype(BF16)
    new_one[...] = first.astype(BF16)
    new_two[...] = second


def cost(tokens, terms, moved):
    return pl.CostEstimate(flops=2 * tokens * terms, bytes_accessed=moved, transcendentals=0)


def gathered(own):
    size = lax.axis_size("ey")

    def turn(block, by):
        return lax.ppermute(block, "ey", [(i, (i + by) % size) for i in range(size)])

    up, down = turn(own, 1), turn(own, -1)
    mine = [own, up, down]
    for _ in range(2, size // 2 - 1):
        up, down = turn(up, 1), turn(down, -1)
        mine += [up, down]
    again, down = lax.optimization_barrier((own, down))
    far = turn(again, size // 2)
    mine[-2:] = [up, down]
    last = [far, turn(up, 1), turn(down, -1)]
    swap = [(0, 1), (1, 0)]
    theirs = [lax.ppermute(jnp.concatenate(g, axis=0), "core", swap) for g in (mine, last)]
    return mine + last + theirs


def shards(grad_out, gates, expert_ids, hidden, down_weight, moment_one, moment_two):
    tokens, width = grad_out.shape
    choices = gates.shape[1]
    replicas, planes = lax.axis_size("edata"), lax.axis_size("tensor")
    groups = lax.axis_size("ey") * 2
    held, capacity = hidden.shape[2], hidden.shape[3]
    rows = held * capacity
    part = width // replicas
    every = groups * tokens

    toks = gathered(
        pl.pallas_call(
            pack_kernel,
            in_specs=[pl.BlockSpec(memory_space=pltpu.HBM)] * 3,
            out_shape=jax.ShapeDtypeStruct((tokens, width + LANES), BF16),
            scratch_shapes=[
                pltpu.VMEM((choices, tokens), jnp.int32),
                pltpu.VMEM((choices, tokens), BF16),
                pltpu.SemaphoreType.DMA((3,)),
            ],
            compiler_params=pltpu.CompilerParams(vmem_limit_bytes=60 * 1024 * 1024),
            name="pack",
        )(grad_out, expert_ids.T, gates.T)
    )
    saved = jnp.transpose(hidden[0], (0, 2, 1, 3)).reshape(groups // 2, 2, rows, LANES)
    weight = down_weight.reshape(held * LANES, width)
    grad_hidden, gate_part, *grads = pl.pallas_call(
        functools.partial(own_kernel, tokens, rows, width, planes, len(toks)),
        out_shape=(
            jax.ShapeDtypeStruct(saved.shape, BF16),
            jax.ShapeDtypeStruct((groups * planes, 1, held * tokens), F32),
        )
        + (jax.ShapeDtypeStruct((part, held * LANES), BF16),) * replicas,
        scratch_shapes=[pltpu.VMEM((every, width + LANES), BF16)],
        compiler_params=PARAMS,
        cost_estimate=cost(every, 2 * width * held * LANES, 8 << 20),
        name="own_tokens",
    )(*toks, weight, saved)

    for step in range(1, replicas):
        to_owner = [(i, (i + step) % replicas) for i in range(replicas)]
        grads[step] = lax.ppermute(grads[step], "edata", to_owner)
    gate_home = lax.all_to_all(gate_part, ("ey", "core", "tensor"), 0, 0, tiled=True)
    flat = (part * held, LANES)
    new_weight, new_one, new_two = pl.pallas_call(
        functools.partial(adam_kernel, part, replicas),
        out_shape=(
            jax.ShapeDtypeStruct(flat, BF16),
            jax.ShapeDtypeStruct(flat, BF16),
            jax.ShapeDtypeStruct(flat, F32),
        ),
        scratch_shapes=[pltpu.VMEM(flat, F32), pltpu.VMEM(flat, F32)],
        compiler_params=PARAMS,
        cost_estimate=cost(part, held * LANES, 8 << 20),
        name="adam",
    )(*grads, weight, moment_one.reshape(flat), moment_two.reshape(flat))
    grad_gates = pl.pallas_call(
        functools.partial(home_kernel, tokens, planes),
        out_shape=jax.ShapeDtypeStruct((choices, tokens), F32),
        compiler_params=PARAMS,
        name="gates_home",
    )(gate_home, expert_ids.T).T
    grad_hidden = jnp.transpose(
        grad_hidden.reshape(1, groups, capacity, held, LANES), (0, 1, 3, 2, 4)
    )
    shape = moment_one.shape
    return (
        grad_hidden, grad_gates, new_weight.reshape(shape), new_one.reshape(shape),
        new_two.reshape(shape),
    )


def solution(mesh):
    replicas, groups, planes = mesh.devices.shape
    fine = Mesh(
        mesh.devices.reshape(replicas, groups // 2, 2, planes), ("edata", "ey", "core", "tensor")
    )
    expert = ("ey", "core")
    block = P(("edata", "ey", "core"), None)
    state = P("edata", expert, "tensor")
    saved = P("edata", None, expert, None, "tensor")
    return jax.shard_map(
        shards,
        mesh=fine,
        in_specs=(block, block, block, saved, P(expert, "tensor", None), state, state),
        out_specs=(saved, block, state, state, state),
        check_vma=False,
    )
```

```python
import functools

import jax
import jax.numpy as jnp
from jax import lax
from jax.experimental import pallas as pl
from jax.experimental.pallas import tpu as pltpu
from jax.sharding import Mesh, PartitionSpec as P

beta_one = 0.9
beta_two = 0.999
adam_eps = 1e-08
learn_rate = 0.01
corr_two = 0.6323045752

F32 = jnp.float32
BF16 = jnp.bfloat16
LANES = 128
PARAMS = pltpu.CompilerParams(vmem_limit_bytes=24 * 1024 * 1024)


def dot(a, b, over, precision=None):
    return lax.dot_general(
        a, b, (((over[0],), (over[1],)), ((), ())), precision=precision, preferred_element_type=F32
    )


def expert_base():
    return ((lax.axis_index("ey") * 2 + lax.axis_index("core")) * 2).astype(F32)


def routed(meta, base, tokens, rows):
    count = meta.shape[0]
    meta = meta.astype(F32)
    ids, gates = meta[:, :8], meta[:, 8:16]
    hits = [ids == base + e for e in range(2)]
    named = [jnp.sum(jnp.where(h, 1.0, 0.0), axis=1, keepdims=True) for h in hits]
    gate = [jnp.sum(jnp.where(h, gates, 0.0), axis=1, keepdims=True) for h in hits]
    lane = lax.broadcasted_iota(jnp.int32, (count, LANES), 1)
    marks = jnp.where(lane == 0, named[0], jnp.where(lane == 1, named[1], 0.0)).astype(BF16)
    row_i = lax.broadcasted_iota(jnp.int32, (count, count), 0)
    col_i = lax.broadcasted_iota(jnp.int32, (count, count), 1)
    earlier = ((row_i // tokens == col_i // tokens) & (col_i < row_i)).astype(F32).astype(BF16)
    rank = dot(earlier, marks, (1, 0))
    block = (lax.broadcasted_iota(jnp.int32, (count, 1), 0) // tokens).astype(F32)
    slot_rows = (count // tokens) * rows
    slot_lane = lax.broadcasted_iota(jnp.int32, (count, slot_rows), 1).astype(F32)
    keys = [
        jnp.where(named[e] > 0.5, block * rows + 2.0 * rank[:, e : e + 1] + e, -1.0)
        for e in range(2)
    ]
    onehot = ((slot_lane == keys[0]) | (slot_lane == keys[1])).astype(F32).astype(BF16)
    return onehot, gate


def by_expert(hid):
    odd = lax.broadcasted_iota(jnp.int32, hid.shape, 0) % 2
    hid = hid.astype(F32)
    return jnp.concatenate(
        [jnp.where(odd == 0, hid, 0.0), jnp.where(odd == 1, hid, 0.0)], axis=1
    ).astype(BF16)


def gate_lanes(gate):
    return jnp.concatenate([jnp.broadcast_to(g, (g.shape[0], LANES)) for g in gate], axis=1)


def pack_kernel(rows_in, ids_in, gates_in, out, ids, gates, sems):
    tokens, width = rows_in.shape
    rows_copy = pltpu.make_async_copy(rows_in, out.at[:, pl.ds(0, width)], sems.at[0])
    ids_copy = pltpu.make_async_copy(ids_in, ids, sems.at[1])
    gates_copy = pltpu.make_async_copy(gates_in, gates, sems.at[2])
    rows_copy.start()
    ids_copy.start()
    gates_copy.start()
    ids_copy.wait()
    gates_copy.wait()
    lying = jnp.concatenate([ids[...].astype(F32), gates[...].astype(F32)], axis=0)
    lying = jnp.concatenate([lying, jnp.zeros((lying.shape[0], LANES - tokens), F32)], axis=1)
    lying = jnp.concatenate([lying, jnp.zeros((LANES - lying.shape[0], LANES), F32)], axis=0)
    out[:, width:] = lying.T[:tokens, :].astype(BF16)
    rows_copy.wait()


def own_kernel(tokens, rows, width, planes, pieces, *refs):
    weight, hid, grad_hidden, gate_part = refs[pieces : pieces + 4]
    grads, toks = refs[pieces + 4 : -1], refs[-1]
    core, line = lax.axis_index("core"), lax.axis_index("ey")
    base = expert_base()
    blocks = grad_hidden.shape[0]
    count = blocks * tokens
    at = 0
    for ref in refs[:pieces]:
        toks[at : at + ref.shape[0], :] = ref[...]
        at += ref.shape[0]
    where = [(line + step) % blocks for step in arrival(blocks)]
    gates_out = None
    scaled = []
    for rel in range(2):
        side = core if rel == 0 else 1 - core
        here = slice(rel * count, (rel + 1) * count)
        onehot, gate = routed(toks[here, width : width + LANES], base, tokens, rows)
        slots = jnp.concatenate([hid[block, side].astype(F32) for block in where], axis=0)
        saved = dot(onehot, by_expert(slots), (1, 0))
        up = dot(toks[here, :width], weight[...], (1, 1))
        scale = gate_lanes(gate)
        scaled.append((scale * saved).astype(BF16))
        picked = dot(onehot, (scale * up).astype(BF16), (0, 0))
        even = lax.broadcasted_iota(jnp.int32, (blocks * rows, LANES), 0) % 2 == 0
        picked = jnp.where(even, picked[:, :LANES], picked[:, LANES:])
        for order, block in enumerate(where):
            grad_hidden[block, side] = picked[order * rows : (order + 1) * rows].astype(BF16)
        prod = saved * up
        lane = lax.broadcasted_iota(jnp.int32, (count, LANES), 1)
        tok = lax.broadcasted_iota(jnp.int32, (count, LANES), 0) % tokens
        spread = jnp.zeros((count, LANES), F32)
        for e in range(2):
            total = jnp.sum(prod[:, e * LANES : (e + 1) * LANES], axis=1, keepdims=True)
            spread = jnp.where(lane == e * tokens + tok, total, spread)
        order = lax.broadcasted_iota(jnp.int32, (2 * blocks, count), 1) // tokens
        away = jnp.zeros_like(order)
        for place, step in enumerate(arrival(blocks)):
            away = jnp.where(order == place, step, away)
        row = lax.broadcasted_iota(jnp.int32, (2 * blocks, count), 0)
        pick = ((line + away) % blocks * 2 + side == row).astype(F32)
        piece = dot(pick, spread, (1, 0), lax.Precision.HIGHEST)
        gates_out = piece if gates_out is None else gates_out + piece
    for group in range(2 * blocks):
        values = gates_out[group : group + 1, : 2 * tokens]
        for plane in range(planes):
            gate_part[group * planes + plane] = values
    scaled = jnp.concatenate(scaled, axis=0)
    part = grads[0].shape[0]
    replicas = len(grads)
    for step, grad in enumerate(grads):
        owner = (lax.axis_index("edata") + step) % replicas
        columns = toks[:, pl.ds(pl.multiple_of(owner * part, LANES), part)]
        grad[...] = dot(columns, scaled, (0, 0)).astype(BF16)


def arrival(blocks):
    steps = [0]
    for away in range(1, blocks // 2):
        steps += [blocks - away, away]
    return steps[:-2] + [blocks // 2] + steps[-2:]


def home_kernel(tokens, planes, arrived, ids, out):
    groups = arrived.shape[0] // planes
    total = jnp.zeros(ids.shape, F32)
    named = ids[...]
    for group in range(groups):
        line = arrived[group * planes]
        for plane in range(1, planes):
            line = line + arrived[group * planes + plane]
        for e in range(2):
            value = line[:, e * tokens : (e + 1) * tokens]
            total = jnp.where(named == group * 2 + e, value, total)
    out[...] = total


def adam_kernel(part, replicas, *refs):
    weight, one, two, new_weight, new_one, new_two, grad_rows, weight_rows = refs[replicas:]
    total = sum(ref[...].astype(F32) for ref in refs[1:replicas]) + refs[0][...].astype(F32)
    column = pl.multiple_of(lax.axis_index("edata") * part, LANES)
    for e in range(2):
        grad_rows[pl.ds(e, part, 2), :] = total[:, e * LANES : (e + 1) * LANES]
        piece = weight[e * LANES : (e + 1) * LANES, pl.ds(column, part)].astype(F32)
        weight_rows[pl.ds(e, part, 2), :] = piece.T
    g = grad_rows[...]
    first = beta_one * one[...].astype(F32) + (1.0 - beta_one) * g
    second = beta_two * two[...] + (1.0 - beta_two) * g * g
    update = first / (jnp.sqrt(second / corr_two) + adam_eps)
    new_weight[...] = (weight_rows[...] - learn_rate * update).astype(BF16)
    new_one[...] = first.astype(BF16)
    new_two[...] = second


def cost(tokens, terms, moved):
    return pl.CostEstimate(flops=2 * tokens * terms, bytes_accessed=moved, transcendentals=0)


def gathered(own):
    size = lax.axis_size("ey")

    def turn(block, by):
        return lax.ppermute(block, "ey", [(i, (i + by) % size) for i in range(size)])

    up, down = turn(own, 1), turn(own, -1)
    mine = [own, up, down]
    for _ in range(2, size // 2 - 1):
        up, down = turn(up, 1), turn(down, -1)
        mine += [up, down]
    half = own.shape[0] // 2
    last = [turn(up[:half], 2), turn(down[half:], -2), turn(up, 1), turn(down, -1)]
    swap = [(0, 1), (1, 0)]
    theirs = [lax.ppermute(jnp.concatenate(g, axis=0), "core", swap) for g in (mine, last)]
    return mine + last + theirs


def shards(grad_out, gates, expert_ids, hidden, down_weight, moment_one, moment_two):
    tokens, width = grad_out.shape
    choices = gates.shape[1]
    replicas, planes = lax.axis_size("edata"), lax.axis_size("tensor")
    groups = lax.axis_size("ey") * 2
    held, capacity = hidden.shape[2], hidden.shape[3]
    rows = held * capacity
    part = width // replicas
    every = groups * tokens

    toks = gathered(
        pl.pallas_call(
            pack_kernel,
            in_specs=[pl.BlockSpec(memory_space=pltpu.HBM)] * 3,
            out_shape=jax.ShapeDtypeStruct((tokens, width + LANES), BF16),
            scratch_shapes=[
                pltpu.VMEM((choices, tokens), jnp.int32),
                pltpu.VMEM((choices, tokens), BF16),
                pltpu.SemaphoreType.DMA((3,)),
            ],
            compiler_params=pltpu.CompilerParams(vmem_limit_bytes=60 * 1024 * 1024),
            name="pack",
        )(grad_out, expert_ids.T, gates.T)
    )
    saved = jnp.transpose(hidden[0], (0, 2, 1, 3)).reshape(groups // 2, 2, rows, LANES)
    weight = down_weight.reshape(held * LANES, width)
    grad_hidden, gate_part, *grads = pl.pallas_call(
        functools.partial(own_kernel, tokens, rows, width, planes, len(toks)),
        out_shape=(
            jax.ShapeDtypeStruct(saved.shape, BF16),
            jax.ShapeDtypeStruct((groups * planes, 1, held * tokens), F32),
        )
        + (jax.ShapeDtypeStruct((part, held * LANES), BF16),) * replicas,
        scratch_shapes=[pltpu.VMEM((every, width + LANES), BF16)],
        compiler_params=PARAMS,
        cost_estimate=cost(every, 2 * width * held * LANES, 8 << 20),
        name="own_tokens",
    )(*toks, weight, saved)

    for step in range(1, replicas):
        to_owner = [(i, (i + step) % replicas) for i in range(replicas)]
        grads[step] = lax.ppermute(grads[step], "edata", to_owner)
    gate_home = lax.all_to_all(gate_part, ("ey", "core", "tensor"), 0, 0, tiled=True)
    flat = (part * held, LANES)
    new_weight, new_one, new_two = pl.pallas_call(
        functools.partial(adam_kernel, part, replicas),
        out_shape=(
            jax.ShapeDtypeStruct(flat, BF16),
            jax.ShapeDtypeStruct(flat, BF16),
            jax.ShapeDtypeStruct(flat, F32),
        ),
        scratch_shapes=[pltpu.VMEM(flat, F32), pltpu.VMEM(flat, F32)],
        compiler_params=PARAMS,
        cost_estimate=cost(part, held * LANES, 8 << 20),
        name="adam",
    )(*grads, weight, moment_one.reshape(flat), moment_two.reshape(flat))
    grad_gates = pl.pallas_call(
        functools.partial(home_kernel, tokens, planes),
        out_shape=jax.ShapeDtypeStruct((choices, tokens), F32),
        compiler_params=PARAMS,
        name="gates_home",
    )(gate_home, expert_ids.T).T
    grad_hidden = jnp.transpose(
        grad_hidden.reshape(1, groups, capacity, held, LANES), (0, 1, 3, 2, 4)
    )
    shape = moment_one.shape
    return (
        grad_hidden, grad_gates, new_weight.reshape(shape), new_one.reshape(shape),
        new_two.reshape(shape),
    )


def solution(mesh):
    replicas, groups, planes = mesh.devices.shape
    fine = Mesh(
        mesh.devices.reshape(replicas, groups // 2, 2, planes), ("edata", "ey", "core", "tensor")
    )
    expert = ("ey", "core")
    block = P(("edata", "ey", "core"), None)
    state = P("edata", expert, "tensor")
    saved = P("edata", None, expert, None, "tensor")
    return jax.shard_map(
        shards,
        mesh=fine,
        in_specs=(block, block, block, saved, P(expert, "tensor", None), state, state),
        out_specs=(saved, block, state, state, state),
        check_vma=False,
    )
```
